32 devices in a mesh: dp: 8 (over z, x), mp: 4 (over y, core).
Axes of the slice: x: 2, y: 2, z: 4, core: 2. Of those that a mesh axis runs over, the one named last changes fastest.
Arguments:
- tokens: bfloat16 [10240, 1024], P(('dp', 'mp')), may hold values from -6 to 6
- visible: int32 [128], P('dp'), may hold values from 20 to 78, as said below
- norm1_gain: float32 [1024], replicated, may hold values from 0.5 to 1.5
- norm1_shift: float32 [1024], replicated, may hold values from -1.5 to 1.5
- qkv_weight: bfloat16 [3, 1024, 1024], P(None, None, 'mp'), may hold values from -0.1875 to 0.1875
- qv_bias: float32 [2, 1024], P(None, 'mp'), may hold values from -1.5 to 1.5
- out_weight: bfloat16 [1024, 1024], P('mp'), may hold values from -0.5 to 0.5
- out_bias: float32 [1024], replicated, may hold values from -1.5 to 1.5
- norm2_gain: float32 [1024], replicated, may hold values from 0.5 to 1.5
- norm2_shift: float32 [1024], replicated, may hold values from -1.5 to 1.5
- fc1_weight: bfloat16 [1024, 4096], P(None, 'mp'), may hold values from -0.1875 to 0.1875
- fc1_bias: float32 [4096], P('mp'), may hold values from -1.5 to 1.5
- fc2_weight: bfloat16 [4096, 1024], P('mp'), may hold values from -0.09375 to 0.09375
- fc2_bias: float32 [1024], replicated, may hold values from -1.5 to 1.5
- dec_weight: bfloat16 [1024, 512], replicated, may hold values from -0.1875 to 0.1875
- decoded_grad: bfloat16 [10240, 512], P(('dp', 'mp')), may hold values from -6 to 6
Outputs:
- latent: bfloat16 [10240, 1024], P(('dp', 'mp'))
- grad_tokens: bfloat16 [10240, 1024], P(('dp', 'mp'))
- grad_norm1_gain: float32 [1024], replicated
- grad_norm1_shift: float32 [1024], replicated
- grad_qkv_weight: float32 [3, 1024, 1024], P(None, 'dp', 'mp')
- grad_qv_bias: float32 [2, 1024], P(None, 'mp')
- grad_out_weight: float32 [1024, 1024], P('mp', 'dp')
- grad_out_bias: float32 [1024], replicated
- grad_norm2_gain: float32 [1024], replicated
- grad_norm2_shift: float32 [1024], replicated
- grad_fc1_weight: float32 [1024, 4096], P('dp', 'mp')
- grad_fc1_bias: float32 [4096], P('mp')
- grad_fc2_weight: float32 [4096, 1024], P('mp', 'dp')
- grad_fc2_bias: float32 [1024], replicated
- grad_dec_weight: float32 [1024, 512], replicated
The draws below stay inside these ranges and needn't reach their ends.
Inputs may be any that keep to these rules, and one draw needn't show every extreme that they name: visible patches of each image, the class token not counted.
All inputs are finite; a program needn't handle non-finite values.
Results may differ from the reference program's by a relative error of at most 0.019.
Values may be sent and summed in bfloat16 or wider, within the bound.
No kernel may reach another device: no remote copies, remote signals or barrier semaphores. Data moves between devices by JAX's collectives and lax.ppermute only.
A program may use at most 128 MiB of HBM per device.

```python
import jax
import jax.numpy as jnp
from jax import lax

D = 1024
H = 16
HD = 64
FF = 4096
DEC = 512
SEQ = 80
IMG_DEV = 16
IMAGES = 128
TOKENS = 10240
N_DP = 8


def draw_visible(key, part):
    key = jax.random.fold_in(key, 7)
    first, second = jax.random.split(key)
    counts = jax.random.randint(first, (IMAGES,), 20, SEQ - 1)
    chosen = jax.random.randint(second, (IMAGES // IMG_DEV, 1), 0, IMG_DEV)
    chosen_mask = lax.broadcasted_iota(jnp.int32, (IMAGES // IMG_DEV, IMG_DEV), 1) == chosen
    counts = jnp.where(chosen_mask.reshape(IMAGES), SEQ - 2, counts)
    return counts.astype(jnp.int32)


def spiked(array, own_key, source, target, parts, factor):
    def block_of(axis_at):
        return (jnp.arange(array.shape[axis_at]) // (array.shape[axis_at] // parts)).reshape((-1,) + (1,) * (array.ndim - 1 - axis_at))

    near = jax.random.permutation(own_key, parts)[block_of(target)]
    second = (block_of(target) + parts // 2) % parts
    return jnp.where((block_of(source) == near) | (block_of(source) == second), factor * array, array)


def steps_of(own_key, extent, pieces, least, high):
    factor_of = 1.0
    for axis_at, parts in pieces:
        draws = jax.random.uniform(jax.random.fold_in(jax.random.fold_in(own_key, 6), axis_at), (parts,), jnp.float32, least / len(pieces), high / len(pieces))
        factor_of = factor_of * jnp.repeat(jnp.exp(draws), extent[axis_at] // parts).reshape((-1,) + (1,) * (len(extent) - 1 - axis_at))
    return factor_of


def noise(stream_key, shape, width, bound, pieces=(), dtype=jnp.bfloat16):
    entries = width * jax.random.normal(stream_key, shape, jnp.float32)
    if pieces:
        entries = entries * steps_of(stream_key, shape, pieces, -0.22, 0.18)
    return jnp.clip(entries, -bound, bound).astype(dtype)


def gaussian_with(own_key, extent, deviation, limit, cuts, heavy, dtype=jnp.bfloat16):
    drawn = deviation * jax.random.normal(own_key, extent, jnp.float32)
    if cuts:
        drawn = drawn * steps_of(own_key, extent, cuts, -0.22, 0.18)
    return jnp.clip(spiked(drawn, jax.random.fold_in(own_key, 3), *heavy), -limit, limit).astype(dtype)


def setup_inputs(seed: int = 0) -> dict:
    key_list = jax.random.split(jax.random.key(seed), 17)
    return {
        "tokens": gaussian_with(key_list[0], (TOKENS, D), 1.0, 6.0, ((0, 32),), (0, 1, 32, 2.75)),
        "visible": draw_visible(jax.random.fold_in(key_list[16], 71), 0),
        "norm1_gain": jnp.clip(1.0 + 0.1 * jax.random.normal(key_list[2], (D,), jnp.float32), 0.5, 1.5),
        "norm1_shift": noise(key_list[3], (D,), 0.3, 1.5, (), jnp.float32),
        "qkv_weight": noise(key_list[4], (3, D, D), D ** -0.5, 0.1875, ((2, 4),)),
        "qv_bias": noise(key_list[5], (2, D), 0.3, 1.5, ((1, 4),), jnp.float32),
        "out_weight": noise(key_list[6], (D, D), (D // 8) ** -0.5, 0.5, ((0, 4),)),
        "out_bias": noise(key_list[7], (D,), 0.3, 1.5, (), jnp.float32),
        "norm2_gain": jnp.clip(1.0 + 0.1 * jax.random.normal(key_list[8], (D,), jnp.float32), 0.5, 1.5),
        "norm2_shift": noise(key_list[9], (D,), 0.3, 1.5, (), jnp.float32),
        "fc1_weight": noise(key_list[10], (D, FF), D ** -0.5, 0.1875, ((1, 4),)),
        "fc1_bias": noise(key_list[11], (FF,), 0.3, 1.5, ((0, 4),), jnp.float32),
        "fc2_weight": noise(key_list[12], (FF, D), FF ** -0.5, 0.09375, ((0, 4),)),
        "fc2_bias": noise(key_list[13], (D,), 0.3, 1.5, (), jnp.float32),
        "dec_weight": noise(key_list[14], (D, DEC), D ** -0.5, 0.1875),
        "decoded_grad": noise(key_list[15], (TOKENS, DEC), 1.0, 6.0, ((0, 32),)),
    }


EPS = 1e-06
HIGHEST_PREC = lax.Precision.HIGHEST

@jax.custom_vjp
def low(v):
    return lax.optimization_barrier(v.astype(jnp.bfloat16)).astype(jnp.float32)

@jax.custom_vjp
def low_back(v):
    return v

def low_keep(v):
    return (low(v), None)

def low_pass(kept, grad):
    return (grad,)

def back_keep(v):
    return (v, None)

def back_low(kept, grad):
    return (low(grad),)
low.defvjp(low_keep, low_pass)
low_back.defvjp(back_keep, back_low)

def layer_norm(values, norm_gain, norm_shift):
    row_mean = lax.optimization_barrier(jnp.mean(values, axis=-1, keepdims=True))
    centered = values - row_mean
    variance = lax.optimization_barrier(jnp.mean(centered * centered, axis=-1, keepdims=True))
    return centered * lax.rsqrt(variance + EPS) * norm_gain + norm_shift

def forward_block(params, in_rows, counts):
    norm1_gain, norm1_shift, qkv_weight, qv_bias, out_weight, out_bias, norm2_gain, norm2_shift, fc1_weight, fc1_bias, fc2_weight, fc2_bias, dec_weight = params
    images = counts.shape[0]
    seq_len = in_rows.shape[0] // images
    head_shape = (images, seq_len, H, HD)
    normed = low(layer_norm(in_rows, norm1_gain, norm1_shift))
    qkv_proj = jnp.einsum('rd,tde->tre', normed, qkv_weight, precision=HIGHEST_PREC)
    queries = low(low_back(qkv_proj[0] + qv_bias[0])).reshape(head_shape)
    keys_low = low(low_back(qkv_proj[1])).reshape(head_shape)
    values_low = low(low_back(qkv_proj[2] + qv_bias[1])).reshape(head_shape)
    scores = low_back(jnp.einsum('bqhd,bkhd->bhqk', queries, keys_low, precision=HIGHEST_PREC) * HD ** (-0.5))
    live_keys = (jnp.arange(seq_len)[None, :] <= counts[:, None])[:, None, None, :]
    scores = jnp.where(live_keys, scores, -1e+30)
    row_top = lax.optimization_barrier(jnp.max(scores, axis=-1, keepdims=True))
    row_exp = jnp.exp(scores - row_top)
    probs = low(row_exp / lax.optimization_barrier(jnp.sum(row_exp, axis=-1, keepdims=True)))
    mixed = jnp.einsum('bhqk,bkhd->bqhd', probs, values_low, precision=HIGHEST_PREC)
    mixed = low(low_back(mixed.reshape(images * seq_len, H * HD)))
    attn = low_back(jnp.dot(mixed, out_weight, precision=HIGHEST_PREC) + out_bias)
    hidden = in_rows + attn
    mid_rows = low(layer_norm(hidden, norm2_gain, norm2_shift))
    preact = low_back(jnp.dot(mid_rows, fc1_weight, precision=HIGHEST_PREC) + fc1_bias)
    activated = low(jax.nn.gelu(preact, approximate=False))
    branch = low_back(jnp.dot(activated, fc2_weight, precision=HIGHEST_PREC) + fc2_bias)
    latent = low(hidden + branch)
    decoded = jnp.dot(latent, dec_weight, precision=HIGHEST_PREC)
    return (decoded, latent)

def reference(tokens, visible, norm1_gain, norm1_shift, qkv_weight, qv_bias, out_weight, out_bias, norm2_gain, norm2_shift, fc1_weight, fc1_bias, fc2_weight, fc2_bias, dec_weight, decoded_grad):
    params = tuple((item.astype(jnp.float32) for item in (norm1_gain, norm1_shift, qkv_weight, qv_bias, out_weight, out_bias, norm2_gain, norm2_shift, fc1_weight, fc1_bias, fc2_weight, fc2_bias, dec_weight)))
    blocks_rows = tokens.astype(jnp.float32).reshape(N_DP, IMG_DEV * SEQ, D)
    blocks_grads = decoded_grad.astype(jnp.float32).reshape(N_DP, IMG_DEV * SEQ, DEC)
    blocks_counts = visible.reshape(N_DP, IMG_DEV)

    def scan_step(totals, block_data):
        block_rows, block_counts, block_grads = block_data

        def block_fn(inner_params, inner_rows):
            return forward_block(inner_params, inner_rows, block_counts)
        decoded, pullback, latent = jax.vjp(block_fn, params, block_rows, has_aux=True)
        param_grads, row_grads = pullback(block_grads)
        totals = jax.tree.map(jnp.add, totals, param_grads)
        return (totals, (latent.astype(jnp.bfloat16), row_grads.astype(jnp.bfloat16)))
    zero_grads = jax.tree.map(jnp.zeros_like, params)
    totals, (latents, row_grads) = lax.scan(scan_step, zero_grads, (blocks_rows, blocks_counts, blocks_grads))
    return (latents.reshape(TOKENS, D), row_grads.reshape(TOKENS, D), totals[0], totals[1], totals[2], totals[3], totals[4], totals[5], totals[6], totals[7], totals[8], totals[9], totals[10], totals[11], totals[12])
```

```python
import functools

import jax
import jax.numpy as jnp
from jax import lax
from jax.experimental import pallas as pl
from jax.experimental.pallas import tpu as pltpu
from jax.sharding import PartitionSpec as P

HD = 64
CORES = 2
EPS = 1e-06
F32 = jnp.float32
BF16 = jnp.bfloat16
MIB = 1 << 20


def dot(lhs, rhs):
    return jnp.dot(lhs, rhs, preferred_element_type=F32)


def dot_nt(lhs, rhs):
    return lax.dot_general(lhs, rhs, (((1,), (1,)), ((), ())), preferred_element_type=F32)


def dot_tn(lhs, rhs):
    return lax.dot_general(lhs, rhs, (((0,), (0,)), ((), ())), preferred_element_type=F32)


def norm_stats(values):
    row_mean = jnp.mean(values, axis=-1, keepdims=True)
    centered = values - row_mean
    variance = jnp.mean(centered * centered, axis=-1, keepdims=True)
    inv = lax.rsqrt(variance + EPS)
    return centered * inv, inv


def norm_back(unit, inv, gain, grad):
    scaled = grad * gain
    first = jnp.mean(scaled, axis=-1, keepdims=True)
    second = jnp.mean(scaled * unit, axis=-1, keepdims=True)
    return inv * (scaled - first - unit * second)


def head_mask(cols, head, dtype):
    lane = lax.broadcasted_iota(jnp.int32, (1, cols), 1)
    return jnp.where((lane >= head * HD) & (lane < (head + 1) * HD), 1.0, 0.0).astype(dtype)


def spread_heads(rows, heads):
    cols = rows.shape[1]
    return jnp.concatenate([rows * head_mask(cols, h, rows.dtype) for h in range(heads)], axis=0)


def fold_heads(stacked, heads):
    seq, cols = stacked.shape[0] // heads, stacked.shape[1]
    total = stacked[:seq] * head_mask(cols, 0, stacked.dtype)
    for h in range(1, heads):
        total = total + stacked[h * seq : (h + 1) * seq] * head_mask(cols, h, stacked.dtype)
    return total


def softmax_rows(spread, keys, count):
    scores = dot_nt(spread, keys) * (HD**-0.5)
    col = lax.broadcasted_iota(jnp.int32, scores.shape, 1)
    scores = jnp.where(col <= count, scores, -1e30)
    top = jnp.max(scores, axis=-1, keepdims=True)
    exps = jnp.exp(scores - top)
    return exps / jnp.sum(exps, axis=-1, keepdims=True)


def norm_kernel(tok_ref, gain_ref, shift_ref, normed_ref):
    unit, _ = norm_stats(tok_ref[...].astype(F32))
    normed_ref[...] = (unit * gain_ref[...] + shift_ref[...]).astype(BF16)


def attn_fwd_kernel(seq, normed_ref, vis_ref, w_ref, b_ref, qkv_ref, mixed_ref):
    rows, cols = mixed_ref.shape
    heads = cols // HD
    for t, bias in ((0, 0), (1, None), (2, 1)):
        part = dot(normed_ref[...], w_ref[t])
        if bias is not None:
            part = part + b_ref[bias : bias + 1, :]
        qkv_ref[t] = part.astype(BF16)
    for i in range(rows // seq):
        at = slice(i * seq, (i + 1) * seq)
        probs = softmax_rows(spread_heads(qkv_ref[0, at, :], heads), qkv_ref[1, at, :], vis_ref[i])
        out = dot(probs.astype(BF16), qkv_ref[2, at, :])
        mixed_ref[at, :] = fold_heads(out, heads).astype(BF16)


def attn_bwd_kernel(
    seq, da_ref, vis_ref, qkv_ref, ow_ref, w_ref, dqkv_ref, dn_ref, bias_ref, dm_ref
):
    rows, cols = dm_ref.shape
    heads = cols // HD
    dm_ref[...] = dot_nt(da_ref[...], ow_ref[...]).astype(BF16)
    for i in range(rows // seq):
        at = slice(i * seq, (i + 1) * seq)
        keys, vals = qkv_ref[1, at, :], qkv_ref[2, at, :]
        spread = spread_heads(qkv_ref[0, at, :], heads)
        probs = softmax_rows(spread, keys, vis_ref[i])
        d_mixed = spread_heads(dm_ref[at, :], heads)
        d_probs = dot_nt(d_mixed, vals)
        inner = jnp.sum(probs * d_probs, axis=-1, keepdims=True)
        d_scores = (probs * (d_probs - inner)).astype(BF16)
        dqkv_ref[0, at, :] = (fold_heads(dot(d_scores, keys), heads) * (HD**-0.5)).astype(BF16)
        dqkv_ref[1, at, :] = (dot_tn(d_scores, spread) * (HD**-0.5)).astype(BF16)
        dqkv_ref[2, at, :] = dot_tn(probs.astype(BF16), d_mixed).astype(BF16)
    dn = dot_nt(dqkv_ref[0], w_ref[0]) + dot_nt(dqkv_ref[1], w_ref[1]) + dot_nt(dqkv_ref[2], w_ref[2])
    dn_ref[...] = dn.astype(dn_ref.dtype)
    bias_ref[0:1, :] = jnp.sum(dqkv_ref[0].astype(F32), axis=0, keepdims=True)
    bias_ref[1:2, :] = jnp.sum(dqkv_ref[2].astype(F32), axis=0, keepdims=True)


def hidden_kernel(parts, *refs):
    mixed, weights = refs[:parts], refs[parts : 2 * parts]
    tok_ref, bias_ref, gain_ref, shift_ref, hidden_ref, mid_ref = refs[2 * parts :]
    attn = dot(mixed[0][...], weights[0][...])
    for m, w in zip(mixed[1:], weights[1:]):
        attn = attn + dot(m[...], w[...])
    hidden = tok_ref[...].astype(F32) + (attn + bias_ref[...])
    hidden_ref[...] = hidden
    unit, _ = norm_stats(hidden)
    mid_ref[...] = (unit * gain_ref[...] + shift_ref[...]).astype(BF16)


def branch_kernel(dg_ref, dec_ref, db_ref):
    db_ref[...] = dot_nt(dg_ref[...], dec_ref[...]).astype(BF16)


def ffn_tile(mid, d_branch, fc1, b1, fc2):
    pre = dot(mid, fc1) + b1
    d_act = dot_nt(d_branch, fc2)
    cdf = 0.5 * (1.0 + lax.erf(pre * (0.5**0.5)))
    slope = cdf + pre * (jnp.exp(-0.5 * (pre * pre)) * 0.3989422804014327)
    return (pre * cdf).astype(BF16), (d_act * slope).astype(BF16)


def ffn_kernel(
    tile, mid0_ref, mid1_ref, db0_ref, db1_ref, fc1_ref, b1_ref, fc2_ref, act_ref, dpre_ref, b1g_ref,
    keep_ref, send_ref, acc_ref,
):
    half = mid0_ref.shape[0]
    mid = jnp.concatenate([mid0_ref[...], mid1_ref[...]], axis=0)
    branch = jnp.concatenate([db0_ref[...], db1_ref[...]], axis=0)
    acc_ref[...] = jnp.zeros_like(acc_ref)

    @pl.loop(0, fc1_ref.shape[1] // tile)
    def _(j):
        at = pl.ds(pl.multiple_of(j * tile, tile), tile)
        act, d_pre = ffn_tile(mid, branch, fc1_ref[:, at], b1_ref[:, at], fc2_ref[at, :])
        act_ref[:, at] = act
        dpre_ref[:, at] = d_pre
        b1g_ref[:, at] = jnp.sum(d_pre.astype(F32), axis=0, keepdims=True)
        acc_ref[...] += dot_nt(d_pre, fc1_ref[:, at])

    keep_ref[...] = acc_ref[:half]
    send_ref[...] = acc_ref[half:].astype(BF16)


def cut_cols(ref, order_ref, cuts):
    width = ref.shape[1] // cuts
    return jnp.concatenate(
        [ref[:, pl.ds(pl.multiple_of(order_ref[p] * width, width), width)] for p in range(cuts)], axis=1
    )


def store_slices(total, outs, at):
    rows, width = total.shape[0], outs[0].shape[2]
    p = 0
    for out in outs:
        for k in range(out.shape[0]):
            out[k, at : at + rows] = total[:, p * width : (p + 1) * width].astype(BF16)
            p += 1


def right_side(refs, order_ref, cuts):
    if cuts:
        return jnp.concatenate([cut_cols(ref, order_ref, cuts) for ref in refs], axis=0)
    return jnp.concatenate([ref[...] for ref in refs], axis=0)


def ffn_grad_kernel(tile, first, last, cuts, others, *refs):
    order_ref, mid0_ref, mid1_ref, db0_ref, db1_ref, fc1_ref, b1_ref, fc2_ref = refs[:8]
    refs = refs[8:]
    if not first:
        prev_ref, refs = refs[0], refs[1:]
    rest, refs = refs[: 6 * others], refs[6 * others :]
    rest = [rest[6 * i : 6 * i + 6] for i in range(others)]
    outs, refs = refs[: 2 if cuts else 1], refs[2 if cuts else 1 :]
    act_ref, b1g_ref = refs[:2]
    half = mid0_ref.shape[0]
    at = tile
    mid = jnp.concatenate([mid0_ref[...], mid1_ref[...]], axis=0)
    branch = jnp.concatenate([db0_ref[...], db1_ref[...]], axis=0)
    act, d_pre = ffn_tile(mid, branch, fc1_ref[:, at], b1_ref[:, at], fc2_ref[at, :])
    act_ref[...] = act
    b1g_ref[...] = jnp.sum(d_pre.astype(F32), axis=0, keepdims=True)
    total = dot_nt(d_pre, fc1_ref[:, at])
    if not first:
        total = total + prev_ref[...]
    if last:
        refs[2][...] = total[:half]
        refs[3][...] = total[half:].astype(BF16)
    else:
        refs[2][...] = total
    acts = jnp.concatenate([act] + [r[4][:, at] for r in rest], axis=0)
    pres = jnp.concatenate([d_pre] + [r[5][:, at] for r in rest], axis=0)
    branches = [db0_ref, db1_ref] + [ref for r in rest for ref in r[2:4]]
    store_slices(dot_tn(acts, right_side(branches, order_ref, cuts)), outs, 0)
    mids = [mid0_ref, mid1_ref] + [ref for r in rest for ref in r[:2]]
    store_slices(dot_tn(pres, right_side(mids, order_ref, cuts)), outs, act.shape[1])


def grad_kernel(takes, parts, cuts, order_ref, *refs):
    outs = refs[2 * parts * len(takes) :]
    at = 0
    for i, take in enumerate(takes):
        lhs = refs[2 * parts * i : 2 * parts * i + parts]
        rhs = refs[2 * parts * i + parts : 2 * parts * (i + 1)]
        right = right_side(rhs, order_ref, cuts)
        for t in take:
            if t is None:
                left = jnp.concatenate([ref[...] for ref in lhs], axis=0)
            else:
                left = jnp.concatenate([ref[t] for ref in lhs], axis=0)
            store_slices(dot_tn(left, right), outs, at)
            at += left.shape[1]


def mlp_kernel(chunks, *refs):
    fc2_ref, acts, keeps, send_ref = refs[0], refs[1 : 1 + chunks], refs[1 + chunks : -1], refs[-1]
    for d in range(chunks):
        tiles = acts[d]
        half = keeps[d].shape[0]
        total, at = None, 0
        for ref in tiles if isinstance(tiles, (list, tuple)) else [tiles]:
            term = dot(ref[...], fc2_ref[at : at + ref.shape[1]])
            total = term if total is None else total + term
            at += ref.shape[1]
        keeps[d][...] = total[:half]
        send_ref[d] = total[half:].astype(BF16)


def mid_back_kernel(sums, *refs):
    arrived, refs = refs[:sums], refs[sums:]
    hidden_ref, dg_ref, dec_ref, gain_ref, dh_ref, da_ref, small_ref = refs
    d_mid = arrived[0][...]
    for ref in arrived[1:]:
        d_mid = d_mid + ref[...].astype(F32)
    unit, inv = norm_stats(hidden_ref[...])
    d_latent = dot_nt(dg_ref[...], dec_ref[...])
    d_hidden = d_latent + norm_back(unit, inv, gain_ref[...], d_mid)
    dh_ref[...] = d_hidden
    d_attn = d_hidden.astype(BF16)
    da_ref[...] = d_attn
    small_ref[0:1, :] = jnp.sum(d_mid * unit, axis=0, keepdims=True)
    small_ref[1:2, :] = jnp.sum(d_mid, axis=0, keepdims=True)
    small_ref[2:3, :] = jnp.sum(d_attn.astype(F32), axis=0, keepdims=True)
    small_ref[3:4, :] = jnp.sum(d_latent.astype(BF16).astype(F32), axis=0, keepdims=True)


def token_back_kernel(sums, *refs):
    arrived, refs = refs[:sums], refs[sums:]
    tok_ref, dh_ref, gain_ref, small2_ref, gt_ref, small_ref = refs
    d_normed = arrived[0][...]
    for ref in arrived[1:]:
        d_normed = d_normed + ref[...].astype(F32)
    unit, inv = norm_stats(tok_ref[...].astype(F32))
    gt_ref[...] = (dh_ref[...] + norm_back(unit, inv, gain_ref[...], d_normed)).astype(BF16)
    small_ref[0:4, :] = small2_ref[...]
    small_ref[4:5, :] = jnp.sum(d_normed * unit, axis=0, keepdims=True)
    small_ref[5:6, :] = jnp.sum(d_normed, axis=0, keepdims=True)


def latent_kernel(sums, parts, *refs):
    order_ref, arrived, refs = refs[0], refs[1 : 1 + sums], refs[1 + sums :]
    hidden_ref, bias_ref, dg_ref, latent_ref, keep_ref, send_ref, low_ref = refs
    total = arrived[0][...]
    for ref in arrived[1:]:
        total = total + ref[...].astype(F32)
    low_ref[...] = (hidden_ref[...] + (total + bias_ref[...])).astype(BF16)
    latent_ref[...] = low_ref[...]
    total = dot_tn(cut_cols(low_ref, order_ref, parts), dg_ref[...])
    width = total.shape[0] // parts
    for p in range(parts // 2):
        keep_ref[p] = total[p * width : (p + 1) * width].astype(BF16)
        q = p + parts // 2
        send_ref[p] = total[q * width : (q + 1) * width].astype(BF16)


def pair_kernel(keep_ref, got_ref, out_ref):
    out_ref[...] = (keep_ref[...].astype(F32) + got_ref[...].astype(F32)).astype(out_ref.dtype)


def crossed_kernel(chunks, got_ref, *refs):
    for d, (keep, out) in enumerate(zip(refs[:chunks], refs[chunks:])):
        out[...] = (keep[...].astype(F32) + got_ref[d].astype(F32)).astype(out.dtype)


def fold_kernel(keep_ref, got_ref, low_ref, send_ref):
    half = low_ref.shape[0]
    low_ref[...] = (keep_ref[:half].astype(F32) + got_ref[:half].astype(F32)).astype(BF16)
    send_ref[...] = (keep_ref[half:].astype(F32) + got_ref[half:].astype(F32)).astype(BF16)


def finish_kernel(flips, keep_ref, got_ref, *outs):
    total = keep_ref[0].astype(F32) + got_ref[0].astype(F32)
    at = 0
    for flip, out in zip(flips, outs):
        size = out.shape[1] if flip else out.shape[0]
        piece = total[at : at + size]
        out[...] = piece.T if flip else piece
        at += size


SMEM = pl.BlockSpec(memory_space=pltpu.SMEM)
VMEM = pl.BlockSpec(memory_space=pltpu.VMEM)
ANY = pl.BlockSpec(memory_space=pl.ANY)


def after_kernel(count, kernel, *refs):
    kernel(*refs[count:])


def like(shape, dtype=BF16):
    return jax.ShapeDtypeStruct(shape, dtype)


class Line:
    def __init__(self):
        self.last = []

    def __call__(self, kernel, outs, *args, after=(), smem=(), limit=16, scratch=(), final=False):
        after = self.last + list(after)
        in_specs = [ANY] * len(after) + [SMEM if i in smem else VMEM for i in range(len(args))]
        grid = {"grid": (1,)} if final else {}
        out_specs = [VMEM] * len(outs)
        if final:
            out_specs = [pl.BlockSpec(o.shape, lambda i, n=len(o.shape): (0,) * n) for o in outs]
        results = pl.pallas_call(
            functools.partial(after_kernel, len(after), kernel),
            out_shape=outs,
            in_specs=in_specs,
            out_specs=out_specs,
            scratch_shapes=list(scratch),
            compiler_params=pltpu.CompilerParams(vmem_limit_bytes=limit * MIB),
            cost_estimate=pl.CostEstimate(flops=1024, bytes_accessed=1024, transcendentals=0),
            **grid,
        )(*after, *args)
        self.last = [min(results, key=lambda r: r.size)]
        return results


class Moves:
    def __init__(self, n_mp, n_dp):
        self.n = {"mp": n_mp, "dp": n_dp}
        self.ny = n_mp // CORES

    def flip(self, value, axis, by):
        return lax.ppermute(value, axis, [(i, i ^ by) for i in range(self.n[axis])])

    def core(self, value):
        return self.flip(value, "mp", 1)

    def y(self, value, by, cross=0):
        pairs = [
            (y * CORES + c, ((y + by) % self.ny) * CORES + (c ^ cross))
            for y in range(self.ny)
            for c in range(CORES)
        ]
        return lax.ppermute(value, "mp", pairs)

    def bits(self, axis):
        return [1 << i for i in range((self.n[axis] - 1).bit_length())]

    def order(self, axis, bits=None):
        flips = [0]
        for bit in reversed(bits or self.bits(axis)):
            flips = flips + [f | bit for f in flips]
        return flips

    def total(self, value, axis, dtype):
        for bit in self.bits(axis):
            low = value.astype(dtype)
            value = low.astype(F32) + self.flip(low, axis, bit).astype(F32)
        return value


class Scatter:
    def __init__(self, line, moves, parts, bits):
        self.line, self.moves, self.bits = line, moves, list(bits)
        self.keep, send = parts
        self.start(send)

    def start(self, send):
        self.got = self.moves.flip(send, "dp", self.bits.pop(0))

    def step(self):
        half = self.keep.shape[0] // 2
        shape = (half,) + self.keep.shape[1:]
        self.keep, send = self.line(fold_kernel, [like(shape), like(shape)], self.keep, self.got)
        self.start(send)

    def finish(self, shapes, flips):
        while self.bits:
            self.step()
        outs = [like(s, F32) for s in shapes]
        return self.line(functools.partial(finish_kernel, flips), outs, self.keep, self.got, final=True)


def shards(
    tokens,
    visible,
    norm1_gain,
    norm1_shift,
    qkv_weight,
    qv_bias,
    out_weight,
    out_bias,
    norm2_gain,
    norm2_shift,
    fc1_weight,
    fc1_bias,
    fc2_weight,
    fc2_bias,
    dec_weight,
    decoded_grad,
):
    n_mp, n_dp = lax.axis_size("mp"), lax.axis_size("dp")
    moves, line = Moves(n_mp, n_dp), Line()
    ny = moves.ny
    rows, width = tokens.shape
    cols = qkv_weight.shape[2]
    units = fc1_weight.shape[1]
    dec = dec_weight.shape[1]
    images = visible.shape[0] // n_mp
    seq = rows // images
    mp_at, dp_at = lax.axis_index("mp"), lax.axis_index("dp")
    y_at, c_at = mp_at // CORES, mp_at % CORES
    places = [(d, e) for d in range(ny) for e in range(CORES)]
    row = lambda v: v.reshape(1, -1)
    gain1, shift1, gain2, shift2 = row(norm1_gain), row(norm1_shift), row(norm2_gain), row(norm2_shift)
    slice_cols = width // n_dp
    cuts = n_dp if slice_cols % 128 == 0 else 0
    dp_bits = moves.bits("dp")
    mp_order = jnp.bitwise_xor(mp_at, jnp.array(moves.order("mp"), jnp.int32))

    def dp_order(bits):
        return jnp.bitwise_xor(dp_at, jnp.array(moves.order("dp", bits), jnp.int32))

    def grad_outs(units_here):
        if cuts:
            return [like((n_dp // 2, units_here, slice_cols))] * 2
        return [like((1, units_here, width))]

    def scatter(parts, bits):
        if not cuts:
            natural = parts[0][0].reshape(-1, n_dp, slice_cols).transpose(1, 0, 2)[dp_order(bits)]
            parts = natural[: n_dp // 2], natural[n_dp // 2 :]
        return Scatter(line, moves, parts, bits)

    counts = {}
    for d, e in places:
        owner = lax.rem(y_at - d + ny, ny) * CORES + (c_at + e) % CORES
        counts[d, e] = lax.dynamic_slice_in_dim(visible, owner * images, images)

    tok, grad, out_w = {0: tokens}, {0: decoded_grad}, {(0, 0): out_weight}
    for d in range(1, ny):
        tok[d] = moves.y(tokens, d)
    for d in range(1, ny):
        grad[d] = moves.y(decoded_grad, d)
    share = cols // n_dp
    out_share = lax.dynamic_slice_in_dim(out_weight, dp_at * share, share)
    for d in range(1, ny):
        block = moves.y(out_share, d)[None]
        for bit in reversed(dp_bits):
            block = jnp.concatenate([block, moves.flip(block, "dp", bit)])
        back = jnp.array([moves.order("dp").index(r) for r in range(n_dp)])
        out_w[d, 0] = block[back[jnp.bitwise_xor(dp_at, jnp.arange(n_dp))]].reshape(cols, width)
    others = moves.core(jnp.stack([out_w[d, 0] for d in range(ny)]))
    for d in range(ny):
        out_w[d, 1] = others[d]

    normed, qkv, mixed, d_branch = {}, {}, {}, {}

    def branch(d, after=()):
        (d_branch[d, 0],) = line(branch_kernel, [like((rows, width))], grad[d], dec_weight, after=after)
        d_branch[d, 1] = moves.core(d_branch[d, 0])

    gathered = {d: {} for d in range(ny)}
    for d in range(ny):
        (normed[d, 0],) = line(norm_kernel, [like((rows, width))], tok[d], gain1, shift1)
        normed[d, 1] = moves.core(normed[d, 0])
        if d == 0:
            branch(0)
        for p in ((d, 0), (d, 1)):
            qkv[p], mixed[p] = line(
                functools.partial(attn_fwd_kernel, seq),
                [like((3, rows, cols)), like((rows, cols))],
                normed[p], counts[p], qkv_weight, qv_bias,
                smem=(1,),
            )
        gathered[d][0, 0] = mixed[d, 0]
        gathered[d][0, 1] = moves.core(mixed[d, 1])
        for s in range(1, ny):
            gathered[(d + s) % ny][s, 0] = moves.y(mixed[d, 0], s)
            gathered[(d + s) % ny][s, 1] = moves.y(mixed[d, 1], s, cross=1)
    hidden, mid = {}, {}

    def to_hidden(d, after=()):
        hidden[d], mid[d, 0] = line(
            functools.partial(hidden_kernel, len(places)),
            [like((rows, width), F32), like((rows, width))],
            *[gathered[d][p] for p in places], *[out_w[p] for p in places],
            tok[d], row(out_bias), gain2, shift2, after=after,
        )
        mid[d, 1] = moves.core(mid[d, 0])

    act, d_pre, fc1_bias_terms, dmid_keep, dmid_send, dmid_far = {}, {}, {}, {}, {}, {}
    b1 = row(fc1_bias)
    far = list(reversed(range(1, ny)))
    for d in far:
        to_hidden(d)
        branch(d)
        act[d], d_pre[d], bias, dmid_keep[d], dmid_send[d] = line(
            functools.partial(ffn_kernel, min(256, units)),
            [
                like((2 * rows, units)),
                like((2 * rows, units)),
                like((1, units), F32),
                like((rows, width), F32),
                like((rows, width)),
            ],
            mid[d, 0], mid[d, 1], d_branch[d, 0], d_branch[d, 1], fc1_weight, b1, fc2_weight,
            scratch=[pltpu.VMEM((2 * rows, width), F32)],
        )
        fc1_bias_terms[d] = bias
        crossed = moves.core(dmid_send[d])
        if d == far[-1]:
            to_hidden(0)
        (both,) = line(pair_kernel, [like((rows, width))], dmid_keep[d], crossed)
        dmid_far[d] = moves.y(both, -d)

    tile = min(512, units)
    steps = units // tile
    acts, biases, fc_sums, carry = [], [], [], []
    for j in range(steps):
        bits = dp_bits
        args = [dp_order(bits), mid[0, 0], mid[0, 1], d_branch[0, 0], d_branch[0, 1], fc1_weight, b1, fc2_weight]
        args += carry
        for d in range(1, ny):
            args += [mid[d, 0], mid[d, 1], d_branch[d, 0], d_branch[d, 1], act[d], d_pre[d]]
        final = j == steps - 1
        n_grads = 2 if cuts else 1
        outs = grad_outs(2 * tile) + [like((2 * rows, tile)), like((1, tile), F32)]
        outs += [like((rows, width), F32), like((rows, width))] if final else [like((2 * rows, width), F32)]
        results = line(
            functools.partial(ffn_grad_kernel, slice(j * tile, (j + 1) * tile), j == 0, final, cuts, ny - 1),
            outs, *args, smem=(0,), limit=24,
        )
        fc_sums.append(scatter(results[:n_grads], bits))
        act_tile, bias, *carry = results[n_grads:]
        acts.append(act_tile)
        biases.append(bias)
    dmid_crossed = moves.core(carry[1])

    terms = [carry[0], dmid_crossed] + [dmid_far[d] for d in range(1, ny)]
    d_hidden, d_attn_own, small2 = line(
        functools.partial(mid_back_kernel, len(terms)),
        [like((rows, width), F32), like((rows, width)), like((4, width), F32)],
        *terms, hidden[0], decoded_grad, dec_weight, gain2,
    )
    d_attn = {(0, 0): d_attn_own, (0, 1): moves.core(d_attn_own)}
    for s in range(1, ny):
        d_attn[s, 0] = moves.y(d_attn_own, s)

    act[0] = acts
    flat, spots = [], []
    for d in range(ny):
        tiles = act[d] if d == 0 else [act[d]]
        spots.append((len(flat), len(flat) + len(tiles)))
        flat += tiles

    def mlp_all(*refs):
        fc2_ref, rest = refs[0], refs[1:]
        groups = [list(rest[a:b]) for a, b in spots]
        mlp_kernel(ny, fc2_ref, *groups, *rest[len(flat) :])

    *mlp_keep, mlp_send = line(
        mlp_all, [like((rows, width), F32)] * ny + [like((ny, rows, width))], fc2_weight, *flat
    )
    mlp_crossed = moves.core(mlp_send)

    dqkv, dn, qv_terms = {}, {}, {}

    def attn_back(p, after=()):
        dqkv[p], dn[p], qv_terms[p] = line(
            functools.partial(attn_bwd_kernel, seq),
            [like((3, rows, cols)), like((rows, width), BF16 if p[1] else F32), like((2, cols), F32)],
            d_attn[p], counts[p], qkv[p], out_weight, qkv_weight,
            smem=(1,), scratch=[pltpu.VMEM((rows, cols), BF16)], after=after,
        )

    attn_back((0, 0))
    fc_sums[0].step()
    mlp_near, *mlp_both = line(
        functools.partial(crossed_kernel, ny),
        [like((rows, width), F32)] + [like((rows, width))] * (ny - 1),
        mlp_crossed, *mlp_keep,
    )
    mlp_far = [moves.y(mlp_both[d - 1], -d) for d in range(1, ny)]
    attn_back((0, 1))
    dn_crossed = moves.core(dn[0, 1])
    for s in fc_sums[1:]:
        s.step()
    dn_far = {}
    for d in far:
        d_attn[d, 1] = moves.core(d_attn[d, 0])
        attn_back((d, 0), after=[dn_crossed])
        attn_back((d, 1))
        crossed = moves.core(dn[d, 1])
        if d == far[0]:
            fc_sums[0].step()
        (both,) = line(pair_kernel, [like((rows, width))], dn[d, 0], crossed)
        dn_far[d] = moves.y(both, -d)

    lhs = [dqkv[p] for p in places]
    rhs = [normed[p] for p in places]
    n_parts = len(places)
    grads = line(
        functools.partial(grad_kernel, [(0, 1)], n_parts, cuts), grad_outs(2 * cols),
        dp_order(dp_bits), *lhs, *rhs, smem=(0,),
    )
    qk_sum = scatter(grads, dp_bits)
    for s in fc_sums[1:]:
        s.step()
    bits = dp_bits[1:2] + dp_bits[:1] + dp_bits[2:]
    grads = line(
        functools.partial(grad_kernel, [(2,), (None,)], n_parts, cuts), grad_outs(2 * cols),
        dp_order(bits), *lhs, *rhs, *[mixed[p] for p in places], *[d_attn[p] for p in places], smem=(0,),
    )
    vo_sum = scatter(grads, bits)

    latent, dec_keep, dec_send = line(
        functools.partial(latent_kernel, ny, n_mp),
        [like((rows, width)), like((n_mp // 2, width // n_mp, dec)), like((n_mp // 2, width // n_mp, dec))],
        mp_order, mlp_near, *mlp_far, hidden[0], row(fc2_bias), decoded_grad,
        smem=(0,), scratch=[pltpu.VMEM((rows, width), BF16)],
    )
    dec_bits = moves.bits("mp")
    got = moves.flip(dec_send, "mp", dec_bits[0])
    fc_grads = [s.finish([(tile, slice_cols), (slice_cols, tile)], (False, True)) for s in fc_sums]
    for bit in dec_bits[1:]:
        half = dec_keep.shape[0] // 2
        shape = (half,) + dec_keep.shape[1:]
        dec_keep, dec_send = line(fold_kernel, [like(shape), like(shape)], dec_keep, got)
        got = moves.flip(dec_send, "mp", bit)

    terms = [dn[0, 0], dn_crossed] + [dn_far[d] for d in range(1, ny)]
    grad_tokens, small = line(
        functools.partial(token_back_kernel, len(terms)),
        [like((rows, width)), like((6, width), F32)],
        *terms, tokens, d_hidden, gain1, small2,
    )

    dec_sum = moves.total(dec_keep.astype(F32) + got.astype(F32), "dp", BF16).astype(BF16)
    for bit in reversed(dec_bits):
        dec_sum = jnp.concatenate([dec_sum, moves.flip(dec_sum, "mp", bit)])
    back = jnp.array([moves.order("mp").index(r) for r in range(n_mp)])
    grad_dec_weight = dec_sum[back[jnp.bitwise_xor(mp_at, jnp.arange(n_mp))]]
    grad_dec_weight = grad_dec_weight.reshape(width, dec).astype(F32)

    small = moves.total(small, "mp", F32).reshape(-1)
    fc1_terms = sum([fc1_bias_terms[d] for d in range(1, ny)], jnp.concatenate(biases, axis=1)).reshape(-1)
    qv_sum = sum(qv_terms[p] for p in places).reshape(-1)
    small = moves.total(jnp.concatenate([small, fc1_terms, qv_sum]), "dp", F32)
    vectors = small[: 6 * width].reshape(6, width)
    grad_fc1_bias = small[6 * width : 6 * width + units]
    grad_qv_bias = small[6 * width + units :].reshape(2, cols)

    q_grad, k_grad = qk_sum.finish([(slice_cols, cols)] * 2, (True, True))
    v_grad, grad_out_weight = vo_sum.finish([(slice_cols, cols), (cols, slice_cols)], (True, False))
    return (
        latent,
        grad_tokens,
        vectors[4],
        vectors[5],
        jnp.stack([q_grad, k_grad, v_grad]),
        grad_qv_bias,
        grad_out_weight,
        vectors[2],
        vectors[0],
        vectors[1],
        jnp.concatenate([g[1] for g in fc_grads], axis=1),
        grad_fc1_bias,
        jnp.concatenate([g[0] for g in fc_grads], axis=0),
        vectors[3],
        grad_dec_weight,
    )


def solution(mesh):
    return jax.shard_map(
        shards,
        mesh=mesh,
        in_specs=(
            P(("dp", "mp"), None),
            P("dp"),
            P(),
            P(),
            P(None, None, "mp"),
            P(None, "mp"),
            P("mp", None),
            P(),
            P(),
            P(),
            P(None, "mp"),
            P("mp"),
            P("mp", None),
            P(),
            P(),
            P(("dp", "mp"), None),
        ),
        out_specs=(
            P(("dp", "mp"), None),
            P(("dp", "mp"), None),
            P(),
            P(),
            P(None, "dp", "mp"),
            P(None, "mp"),
            P("mp", "dp"),
            P(),
            P(),
            P(),
            P("dp", "mp"),
            P("mp"),
            P("mp", "dp"),
            P(),
            P(),
        ),
        check_vma=False,
    )
```

```python
import functools

import jax
import jax.numpy as jnp
from jax import lax
from jax.experimental import pallas as pl
from jax.experimental.pallas import tpu as pltpu
from jax.sharding import PartitionSpec as P

HD = 64
CORES = 2
EPS = 1e-06
F32 = jnp.float32
BF16 = jnp.bfloat16
MIB = 1 << 20


def dot(lhs, rhs):
    return jnp.dot(lhs, rhs, preferred_element_type=F32)


def dot_nt(lhs, rhs):
    return lax.dot_general(lhs, rhs, (((1,), (1,)), ((), ())), preferred_element_type=F32)


def dot_tn(lhs, rhs):
    return lax.dot_general(lhs, rhs, (((0,), (0,)), ((), ())), preferred_element_type=F32)


def total_of(terms):
    return functools.reduce(jnp.add, terms)


def norm_stats(values):
    row_mean = jnp.mean(values, axis=-1, keepdims=True)
    centered = values - row_mean
    variance = jnp.mean(centered * centered, axis=-1, keepdims=True)
    inv = lax.rsqrt(variance + EPS)
    return centered * inv, inv


def norm_back(unit, inv, gain, grad):
    scaled = grad * gain
    first = jnp.mean(scaled, axis=-1, keepdims=True)
    second = jnp.mean(scaled * unit, axis=-1, keepdims=True)
    return inv * (scaled - first - unit * second)


def head_mask(cols, head, dtype):
    lane = lax.broadcasted_iota(jnp.int32, (1, cols), 1)
    return jnp.where((lane >= head * HD) & (lane < (head + 1) * HD), 1.0, 0.0).astype(dtype)


def spread_heads(rows, heads):
    cols = rows.shape[1]
    return jnp.concatenate([rows * head_mask(cols, h, rows.dtype) for h in range(heads)], axis=0)


def fold_heads(stacked, heads):
    seq, cols = stacked.shape[0] // heads, stacked.shape[1]
    total = stacked[:seq] * head_mask(cols, 0, stacked.dtype)
    for h in range(1, heads):
        total = total + stacked[h * seq : (h + 1) * seq] * head_mask(cols, h, stacked.dtype)
    return total


def softmax_rows(spread, keys, count):
    scores = dot_nt(spread, keys) * (HD**-0.5)
    col = lax.broadcasted_iota(jnp.int32, scores.shape, 1)
    scores = jnp.where(col <= count, scores, -1e30)
    top = jnp.max(scores, axis=-1, keepdims=True)
    exps = jnp.exp(scores - top)
    return exps / jnp.sum(exps, axis=-1, keepdims=True)


def norm_kernel(tok_ref, gain_ref, shift_ref, normed_ref):
    unit, _ = norm_stats(tok_ref[...].astype(F32))
    normed_ref[...] = (unit * gain_ref[...] + shift_ref[...]).astype(BF16)


def attn_fwd_kernel(seq, vis_ref, normed_ref, weights, biases, qkv_ref, mixed_ref):
    normed = normed_ref[...]
    rows, cols = normed.shape[0], weights[0].shape[2]
    heads = cols // HD
    for e, (w_ref, b_ref) in enumerate(zip(weights, biases)):
        lanes = slice(e * cols, (e + 1) * cols)
        for t, bias in ((0, 0), (1, None), (2, 1)):
            part = dot(normed, w_ref[t])
            if bias is not None:
                part = part + b_ref[bias : bias + 1, :]
            qkv_ref[t, :, lanes] = part.astype(BF16)

        @pl.loop(0, rows // (2 * seq))
        def _(pair):
            for i in (2 * pair, 2 * pair + 1):
                at = pl.ds(pl.multiple_of(i * seq, 16), seq)
                spread = spread_heads(qkv_ref[0, at, lanes], heads)
                probs = softmax_rows(spread, qkv_ref[1, at, lanes], vis_ref[i])
                out = dot(probs.astype(BF16), qkv_ref[2, at, lanes])
                mixed_ref[at, lanes] = fold_heads(out, heads).astype(BF16)


def attn_bwd_kernel(
    seq, vis_ref, da_ref, qkv_ref, out_ws, weights, normed_ref, dqkv_ref, bias_ref, small_ref, dn_ref, dm_ref
):
    rows, cols = dm_ref.shape[0], weights[0].shape[2]
    heads = cols // HD
    dn = None
    for e, (ow_ref, w_ref) in enumerate(zip(out_ws, weights)):
        lanes = slice(e * cols, (e + 1) * cols)
        dm_ref[:, lanes] = dot_nt(da_ref[...], ow_ref[...]).astype(BF16)

        @pl.loop(0, rows // (2 * seq))
        def _(pair):
            for i in (2 * pair, 2 * pair + 1):
                at = pl.ds(pl.multiple_of(i * seq, 16), seq)
                keys, vals = qkv_ref[1, at, lanes], qkv_ref[2, at, lanes]
                spread = spread_heads(qkv_ref[0, at, lanes], heads)
                probs = softmax_rows(spread, keys, vis_ref[i])
                d_mixed = spread_heads(dm_ref[at, lanes], heads)
                d_probs = dot_nt(d_mixed, vals)
                inner = jnp.sum(probs * d_probs, axis=-1, keepdims=True)
                d_scores = (probs * (d_probs - inner)).astype(BF16)
                d_query = fold_heads(dot(d_scores, keys), heads)
                dqkv_ref[0, at, lanes] = (d_query * (HD**-0.5)).astype(BF16)
                dqkv_ref[1, at, lanes] = (dot_tn(d_scores, spread) * (HD**-0.5)).astype(BF16)
                dqkv_ref[2, at, lanes] = dot_tn(probs.astype(BF16), d_mixed).astype(BF16)

        for t in range(3):
            term = dot_nt(dqkv_ref[t, :, lanes], w_ref[t])
            dn = term if dn is None else dn + term
    dn_ref[...] = dn.astype(dn_ref.dtype)
    small_ref[0:1, :] = jnp.sum(dn * normed_ref[...].astype(F32), axis=0, keepdims=True)
    small_ref[1:2, :] = jnp.sum(dn, axis=0, keepdims=True)
    bias_ref[0:1, :] = jnp.sum(dqkv_ref[0].astype(F32), axis=0, keepdims=True)
    bias_ref[1:2, :] = jnp.sum(dqkv_ref[2].astype(F32), axis=0, keepdims=True)


def hidden_kernel(spot_ref, mixed, weights, tok_ref, bias_ref, gain_ref, shift_ref, hidden_ref, mid_ref):
    attn = None
    for m_ref, cores in zip(mixed, weights):
        size = m_ref.shape[1] // len(cores)
        for e, blocks in enumerate(cores):
            for i, w_ref in enumerate(blocks):
                part = w_ref.shape[0]
                at = e * size
                if len(blocks) > 1:
                    at = at + (spot_ref[0] if i == 0 else 1 - spot_ref[0]) * part
                    cut = m_ref[:, pl.ds(pl.multiple_of(at, part), part)]
                else:
                    cut = m_ref[:, at : at + part]
                term = dot(cut, w_ref[...])
                attn = term if attn is None else attn + term
    hidden = tok_ref[...].astype(F32) + (attn + bias_ref[...])
    hidden_ref[...] = hidden
    unit, _ = norm_stats(hidden)
    mid_ref[...] = (unit * gain_ref[...] + shift_ref[...]).astype(BF16)


def branch_kernel(dg_ref, dec_ref, db_ref):
    db_ref[...] = dot_nt(dg_ref[...], dec_ref[...]).astype(BF16)


def ffn_tile(mid, d_branch, fc1, b1, fc2):
    pre = dot(mid, fc1) + b1
    d_act = dot_nt(d_branch, fc2)
    cdf = 0.5 * (1.0 + lax.erf(pre * (0.5**0.5)))
    slope = cdf + pre * (jnp.exp(-0.5 * (pre * pre)) * 0.3989422804014327)
    return (pre * cdf).astype(BF16), (d_act * slope).astype(BF16)


def ffn_kernel(tile, mid_ref, db_ref, fc1_refs, b1_refs, fc2_refs, acts, d_pres, sums, out_ref, acc_ref):
    mid, branch = mid_ref[...], db_ref[...]
    acc_ref[...] = jnp.zeros_like(acc_ref)
    for e, (fc1_ref, b1_ref, fc2_ref) in enumerate(zip(fc1_refs, b1_refs, fc2_refs)):

        @pl.loop(0, fc1_ref.shape[1] // tile)
        def _(j):
            at = pl.ds(pl.multiple_of(j * tile, tile), tile)
            act, d_pre = ffn_tile(mid, branch, fc1_ref[:, at], b1_ref[:, at], fc2_ref[at, :])
            acts[e][:, at] = act
            d_pres[e][:, at] = d_pre
            sums[e][:, at] = jnp.sum(d_pre.astype(F32), axis=0, keepdims=True)
            acc_ref[...] += dot_nt(d_pre, fc1_ref[:, at])

    out_ref[...] = acc_ref[...].astype(out_ref.dtype)


def cut_cols(ref, order_ref, cuts):
    width = ref.shape[1] // cuts
    return jnp.concatenate(
        [ref[:, pl.ds(pl.multiple_of(order_ref[p] * width, width), width)] for p in range(cuts)], axis=1
    )


def store_slices(total, got, outs, part):
    width = outs[0][0].shape[2]
    p = 0
    for group in outs:
        for k in range(group[part].shape[0]):
            piece = total[:, p * width : (p + 1) * width]
            for ref in got:
                piece = piece + ref[part][p].astype(F32)
            group[part][k] = piece.astype(BF16)
            p += 1


def right_side(refs, order_ref, cuts):
    if cuts:
        return jnp.concatenate([cut_cols(ref, order_ref, cuts) for ref in refs], axis=0)
    return jnp.concatenate([ref[...] for ref in refs], axis=0)


def ffn_grad_kernel(tile, cuts, order_ref, acts, d_pres, branches, mids, got, grads):
    left = jnp.concatenate([ref[:, tile] for ref in acts], axis=0)
    store_slices(dot_tn(left, right_side(branches, order_ref, cuts)), got, grads, 0)
    left = jnp.concatenate([ref[:, tile] for ref in d_pres], axis=0)
    store_slices(dot_tn(left, right_side(mids, order_ref, cuts)), got, grads, 1)


def grad_kernel(e, cuts, takes, order_ref, dqkvs, normed, mixed, d_attn, got, outs):
    part, cols = 0, dqkvs[0].shape[2] // CORES
    lanes = slice(e * cols, (e + 1) * cols)
    right = right_side(normed, order_ref, cuts)
    for t in takes:
        left = jnp.concatenate([ref[t, :, lanes] for ref in dqkvs], axis=0)
        store_slices(dot_tn(left, right), got, outs, part)
        part += 1
    if mixed:
        left = jnp.concatenate([ref[:, lanes] for ref in mixed], axis=0)
        store_slices(dot_tn(left, right_side(d_attn, order_ref, cuts)), got, outs, part)


def mlp_kernel(order_ref, fc2_refs, acts, hidden_ref, bias_ref, dgs, keep_ref, sends, dec_outs, low_ref):
    rows = keep_ref.shape[0]
    for d, cores in enumerate(acts):
        total = total_of([dot(ref[...], fc2_ref[...]) for ref, fc2_ref in zip(cores, fc2_refs)])
        if d == 0:
            keep_ref[...] = total
            total = total + (hidden_ref[...] + bias_ref[...])
        else:
            sends[d - 1][...] = total.astype(BF16)
        low_ref[d * rows : (d + 1) * rows] = total.astype(BF16)
    parts = sum(out.shape[0] for out in dec_outs)
    dg = jnp.concatenate([ref[...] for ref in dgs], axis=0)
    grads = dot_tn(cut_cols(low_ref, order_ref, parts), dg)
    width, p = grads.shape[0] // parts, 0
    for out in dec_outs:
        for k in range(out.shape[0]):
            out[k] = grads[p * width : (p + 1) * width].astype(BF16)
            p += 1


def mid_back_kernel(keep_ref, far, hidden_ref, dg_ref, dec_ref, gain_ref, dh_ref, da_ref, small_ref):
    d_mid = total_of([keep_ref[...]] + [ref[...].astype(F32) for ref in far])
    unit, inv = norm_stats(hidden_ref[...])
    d_latent = dot_nt(dg_ref[...], dec_ref[...])
    d_hidden = d_latent + norm_back(unit, inv, gain_ref[...], d_mid)
    dh_ref[...] = d_hidden
    d_attn = d_hidden.astype(BF16)
    da_ref[...] = d_attn
    small_ref[0:1, :] = jnp.sum(d_mid * unit, axis=0, keepdims=True)
    small_ref[1:2, :] = jnp.sum(d_mid, axis=0, keepdims=True)
    small_ref[2:3, :] = jnp.sum(d_attn.astype(F32), axis=0, keepdims=True)
    small_ref[3:4, :] = jnp.sum(d_latent.astype(BF16).astype(F32), axis=0, keepdims=True)


def token_back_kernel(keep_ref, far, tok_ref, dh_ref, gain_ref, gt_ref):
    d_normed = total_of([keep_ref[...]] + [ref[...].astype(F32) for ref in far])
    unit, inv = norm_stats(tok_ref[...].astype(F32))
    gt_ref[...] = (dh_ref[...] + norm_back(unit, inv, gain_ref[...], d_normed)).astype(BF16)


def latent_kernel(keep_ref, far, hidden_ref, bias_ref, latent_ref):
    total = total_of([keep_ref[...]] + [ref[...].astype(F32) for ref in far])
    latent_ref[...] = (hidden_ref[...] + (total + bias_ref[...])).astype(BF16)


def plain_kernel(in_ref, out_ref):
    out_ref[...] = in_ref[...]


def stack_kernel(first_ref, second_ref, out_ref):
    half = first_ref.shape[0]
    out_ref[:half] = first_ref[...]
    out_ref[half:] = second_ref[...]


def place_kernel(spot_ref, first_ref, second_ref, outs, all_ref):
    half, size = first_ref.shape[0], first_ref.shape[1]
    all_ref[:half] = first_ref[...]
    all_ref[half:] = second_ref[...]
    owner = 0
    for out_ref in outs:
        for k in range(out_ref.shape[0] // size):
            out_ref[k * size : (k + 1) * size] = all_ref[spot_ref[owner]].astype(out_ref.dtype)
            owner += 1


def add_kernel(first_ref, second_ref, out_ref):
    out_ref[...] = (first_ref[...].astype(F32) + second_ref[...].astype(F32)).astype(out_ref.dtype)


def some_rows_kernel(first_ref, second_ref, out_ref):
    rows = second_ref.shape[0]
    out_ref[...] = first_ref[...]
    out_ref[:rows] = first_ref[:rows] + second_ref[...]


def small_kernel(small2_ref, normed_terms, fc1_terms, qv_terms, keep_ref, send_ref):
    for e, out_ref in enumerate((keep_ref, send_ref)):
        out_ref[...] = jnp.zeros_like(out_ref)
        out_ref[0:4, :] = small2_ref[...]
        out_ref[4:6, :] = total_of([ref[...] for ref in normed_terms])
        out_ref[6:7, : fc1_terms[e][0].shape[1]] = total_of([ref[...] for ref in fc1_terms[e]])
        total = total_of([ref[...] for ref in qv_terms])
        cols = total.shape[1] // CORES
        out_ref[7:8, :cols] = total[0:1, e * cols : (e + 1) * cols]
        out_ref[7:8, cols : 2 * cols] = total[1:2, e * cols : (e + 1) * cols]


def tick_kernel(out_ref):
    out_ref[...] = jnp.zeros_like(out_ref)


def fold_kernel(keeps, gots, lows, sends):
    for keep_ref, got_ref, low_ref, send_ref in zip(keeps, gots, lows, sends):
        half = low_ref.shape[0]
        low_ref[...] = (keep_ref[:half].astype(F32) + got_ref[:half].astype(F32)).astype(BF16)
        send_ref[...] = (keep_ref[half:].astype(F32) + got_ref[half:].astype(F32)).astype(BF16)


def last_fold_kernel(pairs, lows, send_ref):
    p = 0
    for (keeps, gots), outs in zip(pairs, lows):
        for keep_ref, got_ref, low_ref in zip(keeps, gots, outs):
            low_ref[...] = (keep_ref[:1].astype(F32) + got_ref[:1].astype(F32)).astype(BF16)
            send_ref[p] = (keep_ref[1].astype(F32) + got_ref[1].astype(F32)).astype(BF16)
            p += 1


def finish_kernel(places, sums, outs):
    lows, got_ref = sums
    for p, (low_ref, (which, flip, at)) in enumerate(zip(lows, places)):
        piece = low_ref[0].astype(F32) + got_ref[p].astype(F32)
        piece = piece.T if flip else piece
        if isinstance(at, int):
            outs[which][at] = piece
        elif at[0] is None:
            outs[which][:, at[1] : at[1] + piece.shape[1]] = piece
        else:
            outs[which][at[0] : at[0] + piece.shape[0]] = piece


SMEM = pl.BlockSpec(memory_space=pltpu.SMEM)
VMEM = pl.BlockSpec(memory_space=pltpu.VMEM)
ANY = pl.BlockSpec(memory_space=pl.ANY)


def like(shape, dtype=BF16):
    return jax.ShapeDtypeStruct(shape, dtype)


def nested_kernel(count, kernel, tree, *refs):
    kernel(*jax.tree.unflatten(tree, refs[count:]))


class Line:
    def __init__(self):
        self.last = []

    def __call__(self, kernel, outs, *args, after=(), smem=(), limit=16, scratch=(), final=False):
        after = self.last + list(after)
        flat = jax.tree.leaves(args)
        out_flat, out_tree = jax.tree.flatten(outs)
        tree = jax.tree.structure((*args, *outs, *scratch))
        smem = [args[i] for i in smem]
        in_specs = [ANY] * len(after) + [SMEM if any(v is w for w in smem) else VMEM for v in flat]
        grid = {"grid": (1,)} if final else {}
        out_specs = [VMEM] * len(out_flat)
        if final:
            out_specs = [pl.BlockSpec(o.shape, lambda i, n=len(o.shape): (0,) * n) for o in out_flat]
        results = pl.pallas_call(
            functools.partial(nested_kernel, len(after), kernel, tree),
            out_shape=out_flat,
            in_specs=in_specs,
            out_specs=out_specs,
            scratch_shapes=list(scratch),
            compiler_params=pltpu.CompilerParams(vmem_limit_bytes=limit * MIB),
            cost_estimate=pl.CostEstimate(flops=1024, bytes_accessed=1024, transcendentals=0),
            **grid,
        )(*after, *flat)
        self.last = [min(results, key=lambda r: r.size)]
        return jax.tree.unflatten(out_tree, results)


class Moves:
    def __init__(self, n_mp, n_dp):
        self.n = {"mp": n_mp, "dp": n_dp}
        self.ny = n_mp // CORES

    def flip(self, value, axis, by):
        return lax.ppermute(value, axis, [(i, i ^ by) for i in range(self.n[axis])])

    def core(self, value):
        return self.flip(value, "mp", 1)

    def y(self, value, by, cross=0):
        pairs = [
            (y * CORES + c, ((y + by) % self.ny) * CORES + (c ^ cross))
            for y in range(self.ny)
            for c in range(CORES)
        ]
        return lax.ppermute(value, "mp", pairs)

    def bits(self, axis):
        return [1 << i for i in range((self.n[axis] - 1).bit_length())]

    def order(self, axis, bits=None):
        flips = [0]
        for bit in reversed(bits or self.bits(axis)):
            flips = flips + [f | bit for f in flips]
        return flips

    def total(self, value, axis, dtype):
        for bit in self.bits(axis):
            low = value.astype(dtype)
            value = low.astype(F32) + self.flip(low, axis, bit).astype(F32)
        return value


class Scatter:

    def __init__(self, line, moves, groups, bits):
        self.line, self.moves, self.bits = line, moves, list(bits)
        self.keep, sends = groups
        self.start(sends)

    def start(self, sends):
        bit = self.bits.pop(0)
        self.got = [self.moves.flip(send, "dp", bit) for send in sends]

    def step(self):
        shapes = [like((v.shape[0] // 2,) + v.shape[1:]) for v in self.keep]
        self.keep, sends = self.line(fold_kernel, [shapes, shapes], self.keep, self.got)
        self.start(sends)


def shards(
    tokens,
    visible,
    norm1_gain,
    norm1_shift,
    qkv_weight,
    qv_bias,
    out_weight,
    out_bias,
    norm2_gain,
    norm2_shift,
    fc1_weight,
    fc1_bias,
    fc2_weight,
    fc2_bias,
    dec_weight,
    decoded_grad,
):
    n_mp, n_dp = lax.axis_size("mp"), lax.axis_size("dp")
    moves, line = Moves(n_mp, n_dp), Line()
    ny = moves.ny
    rows, width = tokens.shape
    cols = qkv_weight.shape[2]
    units = fc1_weight.shape[1]
    dec = dec_weight.shape[1]
    images = visible.shape[0] // n_mp
    seq = rows // images
    mp_at, dp_at = lax.axis_index("mp"), lax.axis_index("dp")
    y_at, c_at = mp_at // CORES, mp_at % CORES
    row = lambda v: v.reshape(1, -1)
    gain1, shift1, gain2, shift2 = row(norm1_gain), row(norm1_shift), row(norm2_gain), row(norm2_shift)
    slice_cols = width // n_dp
    cuts = n_dp if slice_cols % 128 == 0 else 0
    dp_bits = moves.bits("dp")
    mp_order = jnp.bitwise_xor(mp_at, jnp.array(moves.order("mp"), jnp.int32))

    def dp_order(bits=None):
        return jnp.bitwise_xor(dp_at, jnp.array(moves.order("dp", bits), jnp.int32))

    def grad_outs(units_here, e):
        if cuts:
            groups = [n_dp] if e else [n_dp // 2, n_dp // 2]
            return [[like((size, units_here, slice_cols))] * 2 for size in groups]
        return [[like((1, units_here, width))] * 2]

    def scatter(groups, bits):
        if not cuts:
            order = dp_order(bits)
            parts = [v[0].reshape(-1, n_dp, slice_cols).transpose(1, 0, 2)[order] for v in groups[0]]
            groups = [v[: n_dp // 2] for v in parts], [v[n_dp // 2 :] for v in parts]
        return Scatter(line, moves, groups, bits)

    def last_steps(sums):
        for one in sums:
            while len(one.bits) > 1:
                one.step()
        bit = sums[0].bits[0]
        lows = [[like((1,) + v.shape[1:]) for v in one.keep] for one in sums]
        parts = sum(len(group) for group in lows)
        lows, send = line(
            last_fold_kernel, [lows, like((parts,) + lows[0][0].shape[1:])], [(one.keep, one.got) for one in sums]
        )
        return sum(lows, []), moves.flip(send, "dp", bit)

    def finish(sums, shapes, spots):
        outs = [like(shape, F32) for shape in shapes]
        return line(functools.partial(finish_kernel, spots), [outs], sums, final=True)[0]

    counts = {}
    for d in range(ny):
        owner = lax.rem(y_at - d + ny, ny) * CORES + c_at
        counts[d] = lax.dynamic_slice_in_dim(visible, owner * images, images)
    full, wide = like((rows, width)), like((rows, width), F32)
    far = list(reversed(range(1, ny)))

    def tick(*after):
        line(tick_kernel, [like((8, 128))], after=after)

    halved = (cols // 2) % 128 == 0 and n_dp > 1
    near = dp_at % 2
    spot = near.astype(jnp.int32)[None]
    out_part = lax.dynamic_slice_in_dim(out_weight, near * (cols // 2), cols // 2) if halved else out_weight
    out_w = {0: [[out_weight], [moves.core(out_weight)]]}
    for d in range(1, ny):
        pieces = [moves.y(out_part, d)]
        if halved:
            pieces.append(moves.flip(pieces[0], "dp", 1))
        out_w[d] = [pieces, [moves.core(v) for v in pieces]]
    tok, grad = {0: tokens}, {0: decoded_grad}
    for d in range(1, ny):
        tok[d] = moves.y(tokens, d)
    for d in range(1, ny):
        grad[d] = moves.y(decoded_grad, d)
    qkv_w = [qkv_weight, moves.core(qkv_weight)]
    bias_pair = jnp.concatenate([qv_bias.reshape(-1), fc1_bias])
    bias_other = moves.core(bias_pair)
    qv_b = [qv_bias, bias_other[: 2 * cols].reshape(2, cols)]
    b1 = [row(fc1_bias), row(bias_other[2 * cols :])]
    fc1_w = [fc1_weight, moves.core(fc1_weight)]
    fc2_w = [fc2_weight, moves.core(fc2_weight)]
    def spots(axis):
        at = mp_at if axis == "mp" else dp_at
        back = [moves.order(axis).index(r) for r in range(moves.n[axis])]
        return jnp.array(back, jnp.int32)[jnp.bitwise_xor(at, jnp.arange(len(back)))]

    normed, qkv, mixed, d_branch = {}, {}, {}, {}

    def first_norm(d):
        (normed[d],) = line(norm_kernel, [full], tok[d], gain1, shift1)

    def branch(d):
        (d_branch[d],) = line(branch_kernel, [full], grad[d], dec_weight)

    def attend(d):
        qkv[d], mixed[d] = line(
            functools.partial(attn_fwd_kernel, seq),
            [like((3, rows, CORES * cols)), like((rows, CORES * cols))],
            counts[d], normed[d], qkv_w, qv_b,
            smem=(0,),
        )

    gathered = {d: {} for d in range(ny)}

    def send_mixed(d):
        gathered[d][0] = mixed[d]
        for s in range(1, ny):
            gathered[(d + s) % ny][s] = moves.y(mixed[d], s)

    def settle(value):
        return line(plain_kernel, [like(value.shape)], value)[0]

    first_norm(0)
    qkv_w[1] = settle(qkv_w[1])
    attend(0)
    send_mixed(0)
    fc1_w[1] = settle(fc1_w[1])
    branch(0)
    fc2_w[1] = settle(fc2_w[1])
    for d in range(1, ny):
        first_norm(d)
        attend(d)
        send_mixed(d)

    hidden, mid = {}, {}

    def to_hidden(d):
        tick(*[gathered[d][s] for s in range(1, ny)])
        hidden[d], mid[d] = line(
            hidden_kernel, [wide, full],
            spot, [gathered[d][s] for s in range(ny)], [out_w[s] for s in range(ny)],
            tok[d], row(out_bias), gain2, shift2,
            smem=(0,),
        )

    act, d_pre, fc1_sums, dmid = {}, {}, {}, {}
    both, all_d = range(CORES), list(range(ny))

    def feed_forward(d):
        act[d], d_pre[d], fc1_sums[d], dmid[d] = line(
            functools.partial(ffn_kernel, min(512, units)),
            [[like((rows, units))] * CORES, [like((rows, units))] * CORES, [like((1, units), F32)] * CORES]
            + [full if d else wide],
            mid[d], d_branch[d], fc1_w, b1, fc2_w,
            scratch=[pltpu.VMEM((rows, width), F32)],
        )

    for d in far:
        to_hidden(d)
        branch(d)
        feed_forward(d)
        dmid[d] = moves.y(dmid[d], -d)
    to_hidden(0)
    feed_forward(0)

    dec_bits = moves.bits("mp")
    dec_shape = like((n_mp // 2, width // n_mp, dec))
    mlp_keep, mlp_send, (dec_total, dec_send) = line(
        mlp_kernel,
        [wide, [full] * (ny - 1), [dec_shape] * 2],
        mp_order, fc2_w, [act[d] for d in all_d], hidden[0], row(fc2_bias), [grad[d] for d in all_d],
        smem=(0,), limit=24, scratch=[pltpu.VMEM((ny * rows, width), BF16)],
    )
    dec_got = moves.flip(dec_send, "mp", dec_bits[0])

    d_hidden, d_attn_own, small2 = line(
        mid_back_kernel, [wide, full, like((4, width), F32)],
        dmid[0], [dmid[d] for d in range(1, ny)], hidden[0], decoded_grad, dec_weight, gain2,
    )
    d_attn = {0: d_attn_own}
    for s in range(1, ny):
        d_attn[s] = moves.y(d_attn_own, s)
    for bit in dec_bits[1:]:
        half = dec_total.shape[0] // 2
        shape = like((half,) + dec_total.shape[1:])
        (dec_total,), (dec_send,) = line(fold_kernel, [[shape], [shape]], [dec_total], [dec_got])
        dec_got = moves.flip(dec_send, "mp", bit)

    tile = min(512, units)
    steps = units // tile
    swapped = dp_bits[1:2] + dp_bits[:1] + dp_bits[2:]
    fc_sums, fc_got = [], {}
    for e in (1, 0):
        for j in range(steps):
            bits = swapped if j % 2 else dp_bits
            grads = line(
                functools.partial(ffn_grad_kernel, slice(j * tile, (j + 1) * tile), cuts),
                [grad_outs(tile, e)],
                dp_order(bits), [act[d][e] for d in all_d], [d_pre[d][e] for d in all_d],
                [d_branch[d] for d in all_d], [mid[d] for d in all_d], [] if e else [fc_got[j]],
                smem=(0,),
            )[0]
            if e:
                fc_got[j] = [moves.core(v) for v in grads[0]]
            else:
                fc_sums.append(scatter(grads, bits))

    dqkv, dn, qv_terms, small_terms = {}, {}, {}, {}
    dec_todo = list(dp_bits)

    def dec_step(after=()):
        nonlocal dec_total, dec_got
        (dec_total,) = line(add_kernel, [like(dec_total.shape)], dec_total, dec_got, after=after)
        if dec_todo:
            dec_got = moves.flip(dec_total, "dp", dec_todo.pop(0))

    def attn_back(d, after=()):
        dqkv[d], qv_terms[d], small_terms[d], dn[d] = line(
            functools.partial(attn_bwd_kernel, seq),
            [like((3, rows, CORES * cols)), like((2, CORES * cols), F32), like((2, width), F32)]
            + [full if d else wide],
            counts[d], d_attn[d], qkv[d], [w[0] for w in out_w[0]], qkv_w, normed[d],
            smem=(0,), scratch=[pltpu.VMEM((rows, CORES * cols), BF16)], after=after,
        )

    attn_back(0)
    for d in far:
        attn_back(d)
        dn[d] = moves.y(dn[d], -d)
    mlp_far = []
    for d in range(1, ny):
        (send,) = line(plain_kernel, [full], mlp_send[d - 1])
        mlp_far.append(moves.y(send, -d))
    dec_step()
    for s in fc_sums:
        s.step()

    def last_grads(e, takes, more, bits, got=()):
        return line(
            functools.partial(grad_kernel, e, cuts, takes), [grad_outs(cols, e)],
            dp_order(bits), [dqkv[d] for d in all_d], [normed[d] for d in all_d],
            [mixed[d] for d in all_d] if more else [], [d_attn[d] for d in all_d] if more else [], list(got),
            smem=(0,),
        )[0]

    small, small_send = line(
        small_kernel, [like((8, width), F32)] * 2,
        small2, [small_terms[d] for d in all_d], [[fc1_sums[d][e] for d in all_d] for e in both],
        [qv_terms[d] for d in all_d],
    )
    got = moves.core(small_send)
    qk_got = [moves.core(v) for v in last_grads(1, (0, 1), False, dp_bits)[0]]
    (small,) = line(add_kernel, [like(small.shape, F32)], small, got)
    got = moves.flip(small[:6], "mp", moves.bits("mp")[1])
    vo_got = [moves.core(v) for v in last_grads(1, (2,), True, swapped)[0]]
    (small,) = line(some_rows_kernel, [like(small.shape, F32)], small, got)
    for bit in moves.bits("mp")[2:]:
        got = moves.flip(small[:6], "mp", bit)
        (small,) = line(some_rows_kernel, [like(small.shape, F32)], small, got)
    got = moves.flip(small, "dp", dp_bits[0])
    qk_sum = scatter(last_grads(0, (0, 1), False, dp_bits, [qk_got]), dp_bits)
    vo_sum = scatter(last_grads(0, (2,), True, swapped, [vo_got]), swapped)
    (small,) = line(add_kernel, [like(small.shape, F32)], small, got)
    got = moves.flip(small, "dp", dp_bits[1])
    last_fc = last_steps(fc_sums)
    dec_step()
    (latent,) = line(latent_kernel, [full], mlp_keep, mlp_far, hidden[0], row(fc2_bias), final=True)
    qk_sum.step()
    vo_sum.step()
    while dec_todo:
        dec_step()
    terms = [dn[d] for d in range(1, ny)]
    (grad_tokens,) = line(token_back_kernel, [full], dn[0], terms, tokens, d_hidden, gain1, final=True)
    last_sums = last_steps([qk_sum, vo_sum])
    for bit in dp_bits[2:]:
        (small,) = line(add_kernel, [like(small.shape, F32)], small, got)
        got = moves.flip(small, "dp", bit)
    dec_step()
    dec_bits_back = list(reversed(dec_bits))
    for bit in dec_bits_back[:-1]:
        dec_got = moves.flip(dec_total, "mp", bit)
        shape = (2 * dec_total.shape[0],) + dec_total.shape[1:]
        (dec_total,) = line(stack_kernel, [like(shape)], dec_total, dec_got)
    dec_got = moves.flip(dec_total, "mp", dec_bits_back[-1])
    fc1_grad, fc2_grad = finish(
        last_fc,
        [(slice_cols, units), (units, slice_cols)],
        [spot for j in range(steps) for spot in ((1, False, (j * tile, None)), (0, True, (None, j * tile)))],
    )
    (small,) = line(add_kernel, [like(small.shape, F32)], small, got)
    (grad_dec_weight,) = line(
        place_kernel, [[like((width, dec), F32)]], spots("mp"), dec_total, dec_got, smem=(0,), final=True,
        scratch=[pltpu.VMEM((n_mp, width // n_mp, dec), BF16)],
    )[0]
    norm1_shift_grad = small[5]
    norm1_gain_grad = (small[4] - norm1_shift * norm1_shift_grad) / norm1_gain
    grad_qv_bias = small[7, : 2 * cols].reshape(2, cols)
    grad_qkv_weight, grad_out_weight = finish(
        last_sums,
        [(3, slice_cols, cols), (cols, slice_cols)],
        [(0, True, 0), (0, True, 1), (0, True, 2), (1, False, (0, None))],
    )
    return (
        latent,
        grad_tokens,
        norm1_gain_grad,
        norm1_shift_grad,
        grad_qkv_weight,
        grad_qv_bias,
        grad_out_weight,
        small[2],
        small[0],
        small[1],
        fc1_grad,
        small[6, :units],
        fc2_grad,
        small[3],
        grad_dec_weight,
    )


def solution(mesh):
    return jax.shard_map(
        shards,
        mesh=mesh,
        in_specs=(
            P(("dp", "mp"), None),
            P("dp"),
            P(),
            P(),
            P(None, None, "mp"),
            P(None, "mp"),
            P("mp", None),
            P(),
            P(),
            P(),
            P(None, "mp"),
            P("mp"),
            P("mp", None),
            P(),
            P(),
            P(("dp", "mp"), None),
        ),
        out_specs=(
            P(("dp", "mp"), None),
            P(("dp", "mp"), None),
            P(),
            P(),
            P(None, "dp", "mp"),
            P(None, "mp"),
            P("mp", "dp"),
            P(),
            P(),
            P(),
            P("dp", "mp"),
            P("mp"),
            P("mp", "dp"),
            P(),
            P(),
        ),
        check_vma=False,
    )
```

```python
import functools

import jax
import jax.numpy as jnp
from jax import lax
from jax.experimental import pallas as pl
from jax.experimental.pallas import tpu as pltpu
from jax.sharding import PartitionSpec as P

HD = 64
CORES = 2
EPS = 1e-06
F32 = jnp.float32
BF16 = jnp.bfloat16
MIB = 1 << 20


def dot(lhs, rhs):
    return jnp.dot(lhs, rhs, preferred_element_type=F32)


def dot_nt(lhs, rhs):
    return lax.dot_general(lhs, rhs, (((1,), (1,)), ((), ())), preferred_element_type=F32)


def dot_tn(lhs, rhs):
    return lax.dot_general(lhs, rhs, (((0,), (0,)), ((), ())), preferred_element_type=F32)


def total_of(terms):
    return functools.reduce(jnp.add, terms)


def norm_stats(values):
    row_mean = jnp.mean(values, axis=-1, keepdims=True)
    centered = values - row_mean
    variance = jnp.mean(centered * centered, axis=-1, keepdims=True)
    inv = lax.rsqrt(variance + EPS)
    return centered * inv, inv


def norm_back(unit, inv, gain, grad):
    scaled = grad * gain
    first = jnp.mean(scaled, axis=-1, keepdims=True)
    second = jnp.mean(scaled * unit, axis=-1, keepdims=True)
    return inv * (scaled - first - unit * second)


def head_mask(cols, head, dtype):
    lane = lax.broadcasted_iota(jnp.int32, (1, cols), 1)
    return jnp.where((lane >= head * HD) & (lane < (head + 1) * HD), 1.0, 0.0).astype(dtype)


def spread_heads(rows, heads):
    cols = rows.shape[1]
    return jnp.concatenate([rows * head_mask(cols, h, rows.dtype) for h in range(heads)], axis=0)


def fold_heads(stacked, heads):
    seq, cols = stacked.shape[0] // heads, stacked.shape[1]
    total = stacked[:seq] * head_mask(cols, 0, stacked.dtype)
    for h in range(1, heads):
        total = total + stacked[h * seq : (h + 1) * seq] * head_mask(cols, h, stacked.dtype)
    return total


def softmax_rows(spread, keys, count):
    scores = dot_nt(spread, keys) * (HD**-0.5)
    col = lax.broadcasted_iota(jnp.int32, scores.shape, 1)
    scores = jnp.where(col <= count[:, : scores.shape[1]], scores, -1e30)
    top = jnp.max(scores, axis=-1, keepdims=True)
    exps = jnp.exp(scores - top)
    return exps / jnp.sum(exps, axis=-1, keepdims=True)


def norm_kernel(tok_ref, gain_ref, shift_ref, normed_ref):
    unit, _ = norm_stats(tok_ref[...].astype(F32))
    normed_ref[...] = (unit * gain_ref[...] + shift_ref[...]).astype(BF16)


def attn_fwd_kernel(seq, vis_ref, normed_ref, weights, biases, qkv_ref, mixed_ref):
    normed = normed_ref[...]
    rows, cols = normed.shape[0], weights[0].shape[2]
    heads = cols // HD
    for e, (w_ref, b_ref) in enumerate(zip(weights, biases)):
        lanes = slice(e * cols, (e + 1) * cols)
        for t, bias in ((0, 0), (1, None), (2, 1)):
            part = dot(normed, w_ref[t])
            if bias is not None:
                part = part + b_ref[bias : bias + 1, :]
            qkv_ref[t, :, lanes] = part.astype(BF16)

    @pl.loop(0, CORES * rows // (2 * seq))
    def _(step):
        lanes, pair = core_and_pair(step, rows // (2 * seq), cols)
        for i in (2 * pair, 2 * pair + 1):
            at = pl.ds(pl.multiple_of(i * seq, 16), seq)
            spread = spread_heads(qkv_ref[0, at, lanes], heads)
            probs = softmax_rows(spread, qkv_ref[1, at, lanes], vis_ref[pl.ds(i, 1), :])
            out = dot(probs.astype(BF16), qkv_ref[2, at, lanes])
            mixed_ref[at, lanes] = fold_heads(out, heads).astype(BF16)


def core_and_pair(step, pairs, cols):
    core = step // pairs
    return pl.ds(pl.multiple_of(core * cols, cols), cols), step - core * pairs


def attn_bwd_kernel(
    seq, vis_ref, da_ref, qkv_ref, out_ws, weights, normed_ref, dqkv_ref, bias_ref, small_ref, dn_ref, dm_ref,
    acc_ref,
):
    rows, cols = dm_ref.shape[0], weights[0].shape[2]
    heads = cols // HD
    for e, ow_ref in enumerate(out_ws):
        dm_ref[:, e * cols : (e + 1) * cols] = dot_nt(da_ref[...], ow_ref[...]).astype(BF16)

    @pl.loop(0, CORES * rows // (2 * seq))
    def _(step):
        lanes, pair = core_and_pair(step, rows // (2 * seq), cols)
        for i in (2 * pair, 2 * pair + 1):
            at = pl.ds(pl.multiple_of(i * seq, 16), seq)
            keys, vals = qkv_ref[1, at, lanes], qkv_ref[2, at, lanes]
            spread = spread_heads(qkv_ref[0, at, lanes], heads)
            probs = softmax_rows(spread, keys, vis_ref[pl.ds(i, 1), :])
            d_mixed = spread_heads(dm_ref[at, lanes], heads)
            d_probs = dot_nt(d_mixed, vals)
            inner = jnp.sum(probs * d_probs, axis=-1, keepdims=True)
            d_scores = (probs * (d_probs - inner)).astype(BF16)
            d_query = fold_heads(dot(d_scores, keys), heads)
            dqkv_ref[0, at, lanes] = (d_query * (HD**-0.5)).astype(BF16)
            dqkv_ref[1, at, lanes] = (dot_tn(d_scores, spread) * (HD**-0.5)).astype(BF16)
            dqkv_ref[2, at, lanes] = dot_tn(probs.astype(BF16), d_mixed).astype(BF16)

    acc_ref[...] = jnp.zeros_like(acc_ref)

    @pl.loop(0, 3)
    def _(t):
        for e, w_ref in enumerate(weights):
            acc_ref[...] += dot_nt(dqkv_ref[t, :, e * cols : (e + 1) * cols], w_ref[t])

    dn = acc_ref[...]
    dn_ref[...] = dn.astype(dn_ref.dtype)
    small_ref[0:1, :] = jnp.sum(dn * normed_ref[...].astype(F32), axis=0, keepdims=True)
    small_ref[1:2, :] = jnp.sum(dn, axis=0, keepdims=True)
    bias_ref[0:1, :] = jnp.sum(dqkv_ref[0].astype(F32), axis=0, keepdims=True)
    bias_ref[1:2, :] = jnp.sum(dqkv_ref[2].astype(F32), axis=0, keepdims=True)


def hidden_kernel(mixed, weights, tok_ref, bias_ref, gain_ref, shift_ref, hidden_ref, mid_ref):
    attn = None
    for m_ref, cores in zip(mixed, weights):
        size = m_ref.shape[1] // len(cores)
        for e, blocks in enumerate(cores):
            for i, w_ref in enumerate(blocks):
                part = w_ref.shape[0]
                at = e * size
                if len(blocks) > 1:
                    at = at + jnp.bitwise_xor(lax.axis_index("dp") & 1, i) * part
                    cut = m_ref[:, pl.ds(pl.multiple_of(at, part), part)]
                else:
                    cut = m_ref[:, at : at + part]
                term = dot(cut, w_ref[...])
                attn = term if attn is None else attn + term
    hidden = tok_ref[...].astype(F32) + (attn + bias_ref[...])
    hidden_ref[...] = hidden
    unit, _ = norm_stats(hidden)
    mid_ref[...] = (unit * gain_ref[...] + shift_ref[...]).astype(BF16)


def branch_kernel(dg_ref, dec_ref, db_ref):
    db_ref[...] = dot_nt(dg_ref[...], dec_ref[...]).astype(BF16)


def ffn_tile(mid, d_branch, fc1, b1, fc2):
    pre = dot(mid, fc1) + b1
    d_act = dot_nt(d_branch, fc2)
    cdf = 0.5 * (1.0 + lax.erf(pre * (0.5**0.5)))
    slope = cdf + pre * (jnp.exp(-0.5 * (pre * pre)) * 0.3989422804014327)
    return (pre * cdf).astype(BF16), (d_act * slope).astype(BF16)


def ffn_kernel(tile, mid_ref, db_ref, fc1_refs, b1_refs, fc2_refs, acts, d_pres, sums, out_ref, acc_ref):
    mid, branch = mid_ref[...], db_ref[...]
    acc_ref[...] = jnp.zeros_like(acc_ref)
    for e, (fc1_ref, b1_ref, fc2_ref) in enumerate(zip(fc1_refs, b1_refs, fc2_refs)):

        @pl.loop(0, fc1_ref.shape[1] // tile)
        def _(j):
            at = pl.ds(pl.multiple_of(j * tile, tile), tile)
            act, d_pre = ffn_tile(mid, branch, fc1_ref[:, at], b1_ref[:, at], fc2_ref[at, :])
            acts[e][:, at] = act
            d_pres[e][:, at] = d_pre
            sums[e][:, at] = jnp.sum(d_pre.astype(F32), axis=0, keepdims=True)
            acc_ref[...] += dot_nt(d_pre, fc1_ref[:, at])

    out_ref[...] = acc_ref[...].astype(out_ref.dtype)


def cut_cols(ref, axis, flips):
    width, at = ref.shape[1] // len(flips), lax.axis_index(axis)
    starts = [pl.multiple_of(jnp.bitwise_xor(at, flip) * width, width) for flip in flips]
    return jnp.concatenate([ref[:, pl.ds(start, width)] for start in starts], axis=1)


def overlaps(arrays, at, rows):
    first = 0
    for ref in arrays:
        low, high = max(at, first), min(at + rows, first + ref.shape[1])
        if low < high:
            yield ref, slice(low - first, high - first), slice(low - at, high - at)
        first += ref.shape[1]


def store_slices(total, got, outs, at):
    rows, width = total.shape[0], outs[0][0].shape[2]
    p = 0
    for group in outs:
        for k in range(group[0].shape[0]):
            piece = total[:, p * width : (p + 1) * width]
            if got:
                piece = piece + jnp.concatenate([ref[p, here].astype(F32) for ref, here, _ in overlaps(got, at, rows)])
            for ref, here, there in overlaps(group, at, rows):
                ref[k, here] = piece[there].astype(BF16)
            p += 1


def right_side(refs, flips):
    if flips:
        return jnp.concatenate([cut_cols(ref, "dp", flips) for ref in refs], axis=0)
    return jnp.concatenate([ref[...] for ref in refs], axis=0)


def ffn_grad_kernel(tile, flips, acts, d_pres, branches, mids, got, grads):
    left = jnp.concatenate([ref[:, tile] for ref in acts], axis=0)
    store_slices(dot_tn(left, right_side(branches, flips)), got, grads, 0)
    left = jnp.concatenate([ref[:, tile] for ref in d_pres], axis=0)
    store_slices(dot_tn(left, right_side(mids, flips)), got, grads, left.shape[1])


def grad_kernel(e, flips, takes, dqkvs, normed, mixed, d_attn, got, outs):
    at, cols = 0, dqkvs[0].shape[2] // CORES
    lanes = slice(e * cols, (e + 1) * cols)
    right = right_side(normed, flips)
    for t in takes:
        left = jnp.concatenate([ref[t, :, lanes] for ref in dqkvs], axis=0)
        store_slices(dot_tn(left, right), got, outs, at)
        at += cols
    if mixed:
        left = jnp.concatenate([ref[:, lanes] for ref in mixed], axis=0)
        store_slices(dot_tn(left, right_side(d_attn, flips)), got, outs, at)


def mlp_kernel(flips, fc2_refs, acts, hidden_ref, bias_ref, dgs, keep_ref, sends, dec_outs, low_ref):
    rows = keep_ref.shape[0]
    for d, cores in enumerate(acts):
        total = total_of([dot(ref[...], fc2_ref[...]) for ref, fc2_ref in zip(cores, fc2_refs)])
        if d == 0:
            keep_ref[...] = total
            total = total + (hidden_ref[...] + bias_ref[...])
        else:
            sends[d - 1][...] = total.astype(BF16)
        low_ref[d * rows : (d + 1) * rows] = total.astype(BF16)
    dg = jnp.concatenate([ref[...] for ref in dgs], axis=0)
    grads = dot_tn(cut_cols(low_ref, "mp", flips), dg)
    width, p = grads.shape[0] // len(flips), 0
    for out in dec_outs:
        for k in range(out.shape[0]):
            out[k] = grads[p * width : (p + 1) * width].astype(BF16)
            p += 1


def mid_back_kernel(keep_ref, far, hidden_ref, dg_ref, dec_ref, gain_ref, dh_ref, da_ref, small_ref):
    d_mid = total_of([keep_ref[...]] + [ref[...].astype(F32) for ref in far])
    unit, inv = norm_stats(hidden_ref[...])
    d_latent = dot_nt(dg_ref[...], dec_ref[...])
    d_hidden = d_latent + norm_back(unit, inv, gain_ref[...], d_mid)
    dh_ref[...] = d_hidden
    d_attn = d_hidden.astype(BF16)
    da_ref[...] = d_attn
    small_ref[0:1, :] = jnp.sum(d_mid * unit, axis=0, keepdims=True)
    small_ref[1:2, :] = jnp.sum(d_mid, axis=0, keepdims=True)
    small_ref[2:3, :] = jnp.sum(d_attn.astype(F32), axis=0, keepdims=True)
    small_ref[3:4, :] = jnp.sum(d_latent.astype(BF16).astype(F32), axis=0, keepdims=True)


def token_back_kernel(keep_ref, far, tok_ref, dh_ref, gain_ref, gt_ref):
    d_normed = total_of([keep_ref[...]] + [ref[...].astype(F32) for ref in far])
    unit, inv = norm_stats(tok_ref[...].astype(F32))
    gt_ref[...] = (dh_ref[...] + norm_back(unit, inv, gain_ref[...], d_normed)).astype(BF16)


def latent_kernel(keep_ref, far, hidden_ref, bias_ref, latent_ref):
    total = total_of([keep_ref[...]] + [ref[...].astype(F32) for ref in far])
    latent_ref[...] = (hidden_ref[...] + (total + bias_ref[...])).astype(BF16)


def plain_kernel(in_ref, out_ref):
    out_ref[...] = in_ref[...]


def stack_kernel(first_ref, second_ref, out_ref):
    half = first_ref.shape[0]
    out_ref[:half] = first_ref[...]
    out_ref[half:] = second_ref[...]


def place_kernel(axis, first_ref, second_ref, outs, all_ref):
    bits = (all_ref.shape[0] - 1).bit_length()
    half, size = first_ref.shape[0], first_ref.shape[1]
    all_ref[:half] = first_ref[...]
    all_ref[half:] = second_ref[...]
    owner = 0
    for out_ref in outs:
        for k in range(out_ref.shape[0] // size):
            flip = jnp.bitwise_xor(lax.axis_index(axis), owner)
            spot = sum(((flip >> i) & 1) << (bits - 1 - i) for i in range(bits))
            out_ref[k * size : (k + 1) * size] = all_ref[spot].astype(out_ref.dtype)
            owner += 1


def add_kernel(first_ref, second_ref, out_ref):
    out_ref[...] = (first_ref[...].astype(F32) + second_ref[...].astype(F32)).astype(out_ref.dtype)


def some_rows_kernel(first_ref, second_ref, out_ref):
    rows = second_ref.shape[0]
    out_ref[...] = first_ref[...]
    out_ref[:rows] = first_ref[:rows] + second_ref[...]


def small_kernel(small2_ref, normed_terms, fc1_terms, qv_terms, keep_ref, send_ref):
    for e, out_ref in enumerate((keep_ref, send_ref)):
        out_ref[...] = jnp.zeros_like(out_ref)
        out_ref[0:4, :] = small2_ref[...]
        out_ref[4:6, :] = total_of([ref[...] for ref in normed_terms])
        out_ref[6:7, : fc1_terms[e][0].shape[1]] = total_of([ref[...] for ref in fc1_terms[e]])
        total = total_of([ref[...] for ref in qv_terms])
        cols = total.shape[1] // CORES
        out_ref[7:8, :cols] = total[0:1, e * cols : (e + 1) * cols]
        out_ref[7:8, cols : 2 * cols] = total[1:2, e * cols : (e + 1) * cols]


def tick_kernel(out_ref):
    out_ref[...] = jnp.zeros_like(out_ref)


def fold_kernel(keep_ref, gots, low_ref, send_ref):
    half = low_ref.shape[0]
    for ref, here, there in overlaps(gots, 0, keep_ref.shape[1]):
        low_ref[:, there] = (keep_ref[:half, there].astype(F32) + ref[:half, here].astype(F32)).astype(BF16)
        send_ref[:, there] = (keep_ref[half:, there].astype(F32) + ref[half:, here].astype(F32)).astype(BF16)


def finish_kernel(places, sums, outs):
    lows, gots = sums
    for i, (low_ref, pieces) in enumerate(zip(lows, places)):
        total = low_ref[0].astype(F32) + gots[i][0].astype(F32)
        size = total.shape[0] // len(pieces)
        for k, (which, flip, at) in enumerate(pieces):
            piece = total[k * size : (k + 1) * size]
            piece = piece.T if flip else piece
            if isinstance(at, int):
                outs[which][at] = piece
            elif at[0] is None:
                outs[which][:, at[1] : at[1] + piece.shape[1]] = piece
            else:
                outs[which][at[0] : at[0] + size] = piece


def put_exact(value, out_ref, at):
    rows, cols = value.shape[0], value.shape[1] // 2
    high = value.astype(BF16)
    low = (value - high.astype(F32)).astype(BF16)
    for i, part in enumerate((high[:, :cols], high[:, cols:], low[:, :cols], low[:, cols:])):
        out_ref[at + i * rows : at + (i + 1) * rows] = part


def get_exact(ref, at, rows):
    parts = [ref[at + i * rows : at + (i + 1) * rows].astype(F32) for i in range(4)]
    return jnp.concatenate([parts[0] + parts[2], parts[1] + parts[3]], axis=1)


def mix_kernel(keep_ref, got_ref, small_ref, out_ref):
    rows = keep_ref.shape[1]
    out_ref[:rows] = (keep_ref[0].astype(F32) + got_ref[0].astype(F32)).astype(BF16)
    put_exact(small_ref[...], out_ref, rows)


def mix_add_kernel(rows, first_ref, second_ref, out_ref):
    out_ref[:rows] = (first_ref[:rows].astype(F32) + second_ref[:rows].astype(F32)).astype(BF16)
    count = (out_ref.shape[0] - rows) // 4
    put_exact(get_exact(first_ref, rows, count) + get_exact(second_ref, rows, count), out_ref, rows)


def mix_end_kernel(rows, first_ref, second_ref, dec_ref, small_ref):
    dec_ref[0] = (first_ref[:rows].astype(F32) + second_ref[:rows].astype(F32)).astype(BF16)
    count = small_ref.shape[0]
    small_ref[...] = get_exact(first_ref, rows, count) + get_exact(second_ref, rows, count)


VMEM = pl.BlockSpec(memory_space=pltpu.VMEM)
ANY = pl.BlockSpec(memory_space=pl.ANY)


def like(shape, dtype=BF16):
    return jax.ShapeDtypeStruct(shape, dtype)


def nested_kernel(count, kernel, tree, *refs):
    kernel(*jax.tree.unflatten(tree, refs[count:]))


class Line:
    def __init__(self):
        self.last = []

    def __call__(self, kernel, outs, *args, after=(), limit=16, scratch=(), final=False):
        after = self.last + list(after)
        flat = jax.tree.leaves(args)
        out_flat, out_tree = jax.tree.flatten(outs)
        tree = jax.tree.structure((*args, *outs, *scratch))
        in_specs = [ANY] * len(after) + [VMEM] * len(flat)
        grid = {"grid": (1,)} if final else {}
        out_specs = [VMEM] * len(out_flat)
        if final:
            out_specs = [pl.BlockSpec(o.shape, lambda i, n=len(o.shape): (0,) * n) for o in out_flat]
        results = pl.pallas_call(
            functools.partial(nested_kernel, len(after), kernel, tree),
            out_shape=out_flat,
            in_specs=in_specs,
            out_specs=out_specs,
            scratch_shapes=list(scratch),
            compiler_params=pltpu.CompilerParams(vmem_limit_bytes=limit * MIB),
            cost_estimate=pl.CostEstimate(flops=1024, bytes_accessed=1024, transcendentals=0),
            **grid,
        )(*after, *flat)
        self.last = [min(results, key=lambda r: r.size)]
        return jax.tree.unflatten(out_tree, results)


class Moves:
    def __init__(self, n_mp, n_dp):
        self.n = {"mp": n_mp, "dp": n_dp}
        self.ny = n_mp // CORES

    def flip(self, value, axis, by):
        return lax.ppermute(value, axis, [(i, i ^ by) for i in range(self.n[axis])])

    def core(self, value):
        return self.flip(value, "mp", 1)

    def y(self, value, by, cross=0):
        pairs = [
            (y * CORES + c, ((y + by) % self.ny) * CORES + (c ^ cross))
            for y in range(self.ny)
            for c in range(CORES)
        ]
        return lax.ppermute(value, "mp", pairs)

    def bits(self, axis):
        return [1 << i for i in range((self.n[axis] - 1).bit_length())]

    def order(self, axis, bits=None):
        flips = [0]
        for bit in reversed(bits or self.bits(axis)):
            flips = flips + [f | bit for f in flips]
        return flips

    def total(self, value, axis, dtype):
        for bit in self.bits(axis):
            low = value.astype(dtype)
            value = low.astype(F32) + self.flip(low, axis, bit).astype(F32)
        return value


class Scatter:
    def __init__(self, line, moves, groups, bits):
        self.line, self.moves, self.bits = line, moves, list(bits)
        (self.keep,), sends = groups
        self.start(sends)

    def start(self, sends):
        bit = self.bits.pop(0)
        self.got = [self.moves.flip(send, "dp", bit) for send in sends]

    def step(self):
        shape = like((self.keep.shape[0] // 2,) + self.keep.shape[1:])
        self.keep, send = self.line(fold_kernel, [shape, shape], self.keep, self.got)
        self.start([send])


def shards(
    tokens,
    visible,
    norm1_gain,
    norm1_shift,
    qkv_weight,
    qv_bias,
    out_weight,
    out_bias,
    norm2_gain,
    norm2_shift,
    fc1_weight,
    fc1_bias,
    fc2_weight,
    fc2_bias,
    dec_weight,
    decoded_grad,
):
    n_mp, n_dp = lax.axis_size("mp"), lax.axis_size("dp")
    moves, line = Moves(n_mp, n_dp), Line()
    ny = moves.ny
    rows, width = tokens.shape
    cols = qkv_weight.shape[2]
    units = fc1_weight.shape[1]
    dec = dec_weight.shape[1]
    images = visible.shape[0] // n_mp
    seq = rows // images
    mp_at, dp_at = lax.axis_index("mp"), lax.axis_index("dp")
    y_at, c_at = mp_at // CORES, mp_at % CORES
    row = lambda v: v.reshape(1, -1)
    gain1, shift1, gain2, shift2 = row(norm1_gain), row(norm1_shift), row(norm2_gain), row(norm2_shift)
    slice_cols = width // n_dp
    cuts = n_dp if slice_cols % 128 == 0 else 0
    dp_bits = moves.bits("dp")

    def dp_order(bits=None):
        return jnp.bitwise_xor(dp_at, jnp.array(moves.order("dp", bits), jnp.int32))

    def flips(bits=None):
        return moves.order("dp", bits) if cuts else []

    def grad_outs(rows_here, e, parts):
        cut_up = lambda size, n: [like((size, rows_here // n, slice_cols))] * n
        if cuts:
            return [cut_up(n_dp, parts)] if e else [cut_up(n_dp // 2, 1), cut_up(n_dp // 2, parts)]
        return [[like((1, rows_here // n, width))] * n for n in [parts if e else 1]]

    def scatter(groups, bits, parts):
        if not cuts:
            natural = groups[0][0][0]
            slices = natural.reshape(-1, n_dp, slice_cols).transpose(1, 0, 2)[dp_order(bits)]
            groups = [slices[: n_dp // 2]], jnp.split(slices[n_dp // 2 :], parts, axis=1)
        return Scatter(line, moves, groups, bits)

    def finish(sums, shapes, spots):
        outs = [like(shape, F32) for shape in shapes]
        return line(functools.partial(finish_kernel, spots), [outs], sums, final=True)[0]

    counts = {}
    for d in range(ny):
        owner = lax.rem(y_at - d + ny, ny) * CORES + c_at
        own = lax.dynamic_slice_in_dim(visible, owner * images, images)
        counts[d] = jnp.broadcast_to(own[:, None], (images, 128))
    full, wide = like((rows, width)), like((rows, width), F32)
    far = list(reversed(range(1, ny)))

    def tick(*after):
        line(tick_kernel, [like((8, 128))], after=after)

    halved = (cols // 2) % 128 == 0 and n_dp > 1
    near = dp_at % 2
    out_part = lax.dynamic_slice_in_dim(out_weight, near * (cols // 2), cols // 2) if halved else out_weight
    out_w = {0: [[out_weight], [moves.core(out_weight)]]}
    for d in range(1, ny):
        pieces = [moves.y(out_part, d)]
        if halved:
            pieces.append(moves.flip(pieces[0], "dp", 1))
        out_w[d] = [pieces, [moves.core(v) for v in pieces]]
    tok, grad = {0: tokens}, {0: decoded_grad}
    for d in range(1, ny):
        tok[d] = moves.y(tokens, d)
    for d in range(1, ny):
        grad[d] = moves.y(decoded_grad, d)
    qkv_w = [qkv_weight, moves.core(qkv_weight)]
    bias_pair = jnp.concatenate([qv_bias.reshape(-1), fc1_bias])
    bias_other = moves.core(bias_pair)
    qv_b = [qv_bias, bias_other[: 2 * cols].reshape(2, cols)]
    b1 = [row(fc1_bias), row(bias_other[2 * cols :])]
    fc1_w = [fc1_weight, moves.core(fc1_weight)]
    fc2_w = [fc2_weight, moves.core(fc2_weight)]
    normed, qkv, mixed, d_branch = {}, {}, {}, {}

    def first_norm(d):
        (normed[d],) = line(norm_kernel, [full], tok[d], gain1, shift1)

    def branch(d):
        (d_branch[d],) = line(branch_kernel, [full], grad[d], dec_weight)

    def attend(d):
        qkv[d], mixed[d] = line(
            functools.partial(attn_fwd_kernel, seq),
            [like((3, rows, CORES * cols)), like((rows, CORES * cols))],
            counts[d], normed[d], qkv_w, qv_b,
        )

    gathered = {d: {} for d in range(ny)}

    def send_mixed(d):
        gathered[d][0] = mixed[d]
        for s in range(1, ny):
            gathered[(d + s) % ny][s] = moves.y(mixed[d], s)

    def settle(value):
        return line(plain_kernel, [like(value.shape)], value)[0]

    first_norm(0)
    qkv_w[1] = settle(qkv_w[1])
    attend(0)
    send_mixed(0)
    fc1_w[1] = settle(fc1_w[1])
    branch(0)
    fc2_w[1] = settle(fc2_w[1])
    for d in range(1, ny):
        first_norm(d)
        attend(d)
        send_mixed(d)

    hidden, mid = {}, {}

    def to_hidden(d):
        tick(*[gathered[d][s] for s in range(1, ny)])
        hidden[d], mid[d] = line(
            hidden_kernel, [wide, full],
            [gathered[d][s] for s in range(ny)], [out_w[s] for s in range(ny)],
            tok[d], row(out_bias), gain2, shift2,
        )

    act, d_pre, fc1_sums, dmid = {}, {}, {}, {}
    both, all_d = range(CORES), list(range(ny))

    def feed_forward(d):
        act[d], d_pre[d], fc1_sums[d], dmid[d] = line(
            functools.partial(ffn_kernel, min(512, units)),
            [[like((rows, units))] * CORES, [like((rows, units))] * CORES, [like((1, units), F32)] * CORES]
            + [full if d else wide],
            mid[d], d_branch[d], fc1_w, b1, fc2_w,
            scratch=[pltpu.VMEM((rows, width), F32)],
        )

    for d in far:
        to_hidden(d)
        branch(d)
        feed_forward(d)
        dmid[d] = moves.y(dmid[d], -d)
    to_hidden(0)
    feed_forward(0)

    tile = min(512, units)
    steps = units // tile
    late_x = dp_bits[1:] + dp_bits[:1]
    tile_bits = [late_x if j % 2 else dp_bits for j in range(steps)]
    fc_sums, fc_got = [], {}

    def ffn_grads(e, j, parts):
        groups = line(
            functools.partial(ffn_grad_kernel, slice(j * tile, (j + 1) * tile), flips(tile_bits[j])),
            [grad_outs(2 * tile, e, parts)],
            [act[d][e] for d in all_d], [d_pre[d][e] for d in all_d],
            [d_branch[d] for d in all_d], [mid[d] for d in all_d], [] if e else fc_got[j],
        )[0]
        if e:
            fc_got[j] = [moves.core(v) for v in groups[0]]
        else:
            fc_sums.append(scatter(groups, tile_bits[j], parts))

    dec_bits = moves.bits("mp")
    dec_shape = like((n_mp // 2, width // n_mp, dec))
    mlp_keep, mlp_send, (dec_total, dec_send) = line(
        functools.partial(mlp_kernel, moves.order("mp")),
        [wide, [full] * (ny - 1), [dec_shape] * 2],
        fc2_w, [act[d] for d in all_d], hidden[0], row(fc2_bias), [grad[d] for d in all_d],
        limit=24, scratch=[pltpu.VMEM((ny * rows, width), BF16)],
    )
    dec_got = moves.flip(dec_send, "mp", dec_bits[0])

    d_hidden, d_attn_own, small2 = line(
        mid_back_kernel, [wide, full, like((4, width), F32)],
        dmid[0], [dmid[d] for d in range(1, ny)], hidden[0], decoded_grad, dec_weight, gain2,
    )
    d_attn = {0: d_attn_own}
    for s in range(1, ny):
        d_attn[s] = moves.y(d_attn_own, s)
    for bit in dec_bits[1:]:
        shape = like((dec_total.shape[0] // 2,) + dec_total.shape[1:])
        dec_total, dec_send = line(fold_kernel, [shape, shape], dec_total, [dec_got])
        if bit != dec_bits[-1]:
            dec_got = moves.flip(dec_send, "mp", bit)
    for e in (1, 0):
        for j in range(steps):
            ffn_grads(e, j, 2)

    dqkv, dn, qv_terms, small_terms = {}, {}, {}, {}

    def attn_back(d, after=()):
        dqkv[d], qv_terms[d], small_terms[d], dn[d] = line(
            functools.partial(attn_bwd_kernel, seq),
            [like((3, rows, CORES * cols)), like((2, CORES * cols), F32), like((2, width), F32)]
            + [full if d else wide],
            counts[d], d_attn[d], qkv[d], [w[0] for w in out_w[0]], qkv_w, normed[d],
            scratch=[pltpu.VMEM((rows, CORES * cols), BF16), pltpu.VMEM((rows, width), F32)], after=after,
        )

    attn_back(0)
    held = lax.optimization_barrier((dec_send, dqkv[0]))
    dec_got = moves.flip(held[0], "mp", dec_bits[-1])
    for d in far:
        attn_back(d)

    def last_grads(e, got=()):
        return line(
            functools.partial(grad_kernel, e, flips(), (0, 1, 2)), [grad_outs(4 * cols, e, 1)],
            [dqkv[d] for d in all_d], [normed[d] for d in all_d],
            [mixed[d] for d in all_d], [d_attn[d] for d in all_d], list(got),
        )[0]

    small, small_send = line(
        small_kernel, [like((8, width), F32)] * 2,
        small2, [small_terms[d] for d in all_d], [[fc1_sums[d][e] for d in all_d] for e in both],
        [qv_terms[d] for d in all_d], after=[dec_got],
    )
    got = moves.core(small_send)
    send = last_grads(1)[0]
    (small,) = line(add_kernel, [like(small.shape, F32)], small, got)
    got = moves.flip(small[:6], "mp", moves.bits("mp")[1])
    fc_sums[0].step()
    (small,) = line(some_rows_kernel, [like(small.shape, F32)], small, got)
    for bit in moves.bits("mp")[2:]:
        got = moves.flip(small[:6], "mp", bit)
        (small,) = line(some_rows_kernel, [like(small.shape, F32)], small, got)
    dec_rows = dec_total.shape[1]
    (mix,) = line(mix_kernel, [like((dec_rows + 4 * small.shape[0], dec))], dec_total, dec_got, small)
    mix_todo = dp_bits[1:] + dp_bits[:1]
    mix_got = moves.flip(mix, "dp", mix_todo.pop(0))

    def mix_step():
        nonlocal mix, mix_got
        (mix,) = line(functools.partial(mix_add_kernel, dec_rows), [like(mix.shape)], mix, mix_got)
        mix_got = moves.flip(mix, "dp", mix_todo.pop(0))

    for s in fc_sums[1:]:
        s.step()
    *held, _ = lax.optimization_barrier((*send, fc_sums[-1].keep))
    crossed = [moves.core(v) for v in held]
    mix_step()
    last_sum = scatter(last_grads(0, crossed), dp_bits, 1)
    for d in range(1, ny):
        (send,) = line(plain_kernel, [full], dn[d])
        dn[d] = moves.y(send, -d)
    fc_sums[0].step()
    while mix_todo:
        mix_step()
    terms = [dn[d] for d in range(1, ny)]
    (grad_tokens,) = line(token_back_kernel, [full], dn[0], terms, tokens, d_hidden, gain1, final=True)
    mlp_far = []
    for d in range(1, ny):
        (send,) = line(plain_kernel, [full], mlp_send[d - 1])
        mlp_far.append(moves.y(send, -d))
    last_sum.step()
    for s in fc_sums[1:]:
        s.step()
    dec_total, small = line(
        functools.partial(mix_end_kernel, dec_rows), [like((1, dec_rows, dec)), like(small.shape, F32)], mix, mix_got
    )
    dec_bits_back = list(reversed(dec_bits))
    for bit in dec_bits_back[:-1]:
        dec_got = moves.flip(dec_total, "mp", bit)
        shape = (2 * dec_total.shape[0],) + dec_total.shape[1:]
        (dec_total,) = line(stack_kernel, [like(shape)], dec_total, dec_got)
    dec_got = moves.flip(dec_total, "mp", dec_bits_back[-1])
    while last_sum.bits:
        last_sum.step()
    for s in fc_sums:
        while s.bits:
            s.step()
    fc1_grad, fc2_grad = finish(
        ([s.keep for s in fc_sums], [s.got[0] for s in fc_sums]),
        [(slice_cols, units), (units, slice_cols)],
        [[(1, False, (j * tile, None)), (0, True, (None, j * tile))] for j in range(steps)],
    )
    (grad_dec_weight,) = line(
        functools.partial(place_kernel, "mp"), [[like((width, dec), F32)]], dec_total, dec_got, final=True,
        scratch=[pltpu.VMEM((n_mp, width // n_mp, dec), BF16)],
    )[0]
    (latent,) = line(latent_kernel, [full], mlp_keep, mlp_far, hidden[0], row(fc2_bias), final=True)
    norm1_shift_grad = small[5]
    norm1_gain_grad = (small[4] - norm1_shift * norm1_shift_grad) / norm1_gain
    grad_qv_bias = small[7, : 2 * cols].reshape(2, cols)
    grad_qkv_weight, grad_out_weight = finish(
        ([last_sum.keep], last_sum.got),
        [(3, slice_cols, cols), (cols, slice_cols)],
        [[(0, True, 0), (0, True, 1), (0, True, 2), (1, False, (0, None))]],
    )
    return (
        latent,
        grad_tokens,
        norm1_gain_grad,
        norm1_shift_grad,
        grad_qkv_weight,
        grad_qv_bias,
        grad_out_weight,
        small[2],
        small[0],
        small[1],
        fc1_grad,
        small[6, :units],
        fc2_grad,
        small[3],
        grad_dec_weight,
    )


def solution(mesh):
    return jax.shard_map(
        shards,
        mesh=mesh,
        in_specs=(
            P(("dp", "mp"), None),
            P("dp"),
            P(),
            P(),
            P(None, None, "mp"),
            P(None, "mp"),
            P("mp", None),
            P(),
            P(),
            P(),
            P(None, "mp"),
            P("mp"),
            P("mp", None),
            P(),
            P(),
            P(("dp", "mp"), None),
        ),
        out_specs=(
            P(("dp", "mp"), None),
            P(("dp", "mp"), None),
            P(),
            P(),
            P(None, "dp", "mp"),
            P(None, "mp"),
            P("mp", "dp"),
            P(),
            P(),
            P(),
            P("dp", "mp"),
            P("mp"),
            P("mp", "dp"),
            P(),
            P(),
        ),
        check_vma=False,
    )
```

```python
import functools

import jax
import jax.numpy as jnp
from jax import lax
from jax.experimental import pallas as pl
from jax.experimental.pallas import tpu as pltpu
from jax.sharding import PartitionSpec as P

HD = 64
CORES = 2
EPS = 1e-06
F32 = jnp.float32
BF16 = jnp.bfloat16
MIB = 1 << 20


def dot(lhs, rhs):
    return jnp.dot(lhs, rhs, preferred_element_type=F32)


def dot_nt(lhs, rhs):
    return lax.dot_general(lhs, rhs, (((1,), (1,)), ((), ())), preferred_element_type=F32)


def dot_tn(lhs, rhs):
    return lax.dot_general(lhs, rhs, (((0,), (0,)), ((), ())), preferred_element_type=F32)


def total_of(terms):
    return functools.reduce(jnp.add, terms)


def norm_stats(values):
    row_mean = jnp.mean(values, axis=-1, keepdims=True)
    centered = values - row_mean
    variance = jnp.mean(centered * centered, axis=-1, keepdims=True)
    inv = lax.rsqrt(variance + EPS)
    return centered * inv, inv


def norm_back(unit, inv, gain, grad):
    scaled = grad * gain
    first = jnp.mean(scaled, axis=-1, keepdims=True)
    second = jnp.mean(scaled * unit, axis=-1, keepdims=True)
    return inv * (scaled - first - unit * second)


def head_mask(cols, head, dtype):
    lane = lax.broadcasted_iota(jnp.int32, (1, cols), 1)
    return jnp.where((lane >= head * HD) & (lane < (head + 1) * HD), 1.0, 0.0).astype(dtype)


def spread_heads(rows, heads):
    cols = rows.shape[1]
    return jnp.concatenate([rows * head_mask(cols, h, rows.dtype) for h in range(heads)], axis=0)


def fold_heads(stacked, heads):
    seq, cols = stacked.shape[0] // heads, stacked.shape[1]
    total = stacked[:seq] * head_mask(cols, 0, stacked.dtype)
    for h in range(1, heads):
        total = total + stacked[h * seq : (h + 1) * seq] * head_mask(cols, h, stacked.dtype)
    return total


def softmax_rows(spread, keys, count):
    scores = dot_nt(spread, keys) * (HD**-0.5)
    col = lax.broadcasted_iota(jnp.int32, scores.shape, 1)
    scores = jnp.where(col <= count[:, : scores.shape[1]], scores, -1e30)
    top = jnp.max(scores, axis=-1, keepdims=True)
    exps = jnp.exp(scores - top)
    return exps / jnp.sum(exps, axis=-1, keepdims=True)


def norm_kernel(tok_ref, gain_ref, shift_ref, normed_ref):
    unit, _ = norm_stats(tok_ref[...].astype(F32))
    normed_ref[...] = (unit * gain_ref[...] + shift_ref[...]).astype(BF16)


def attn_fwd_kernel(seq, vis_ref, normed_ref, weights, biases, qkv_ref, mixed_ref):
    normed = normed_ref[...]
    rows, cols = normed.shape[0], weights[0].shape[2]
    heads = cols // HD
    for e, (w_ref, b_ref) in enumerate(zip(weights, biases)):
        lanes = slice(e * cols, (e + 1) * cols)
        for t, bias in ((0, 0), (1, None), (2, 1)):
            part = dot(normed, w_ref[t])
            if bias is not None:
                part = part + b_ref[bias : bias + 1, :]
            qkv_ref[t, :, lanes] = part.astype(BF16)

    @pl.loop(0, CORES * rows // (2 * seq))
    def _(step):
        lanes, pair = core_and_pair(step, rows // (2 * seq), cols)
        for i in (2 * pair, 2 * pair + 1):
            at = pl.ds(pl.multiple_of(i * seq, 16), seq)
            spread = spread_heads(qkv_ref[0, at, lanes], heads)
            probs = softmax_rows(spread, qkv_ref[1, at, lanes], vis_ref[pl.ds(i, 1), :])
            out = dot(probs.astype(BF16), qkv_ref[2, at, lanes])
            mixed_ref[at, lanes] = fold_heads(out, heads).astype(BF16)


def core_and_pair(step, pairs, cols):
    core = step // pairs
    return pl.ds(pl.multiple_of(core * cols, cols), cols), step - core * pairs


def attn_bwd_kernel(
    seq, vis_ref, da_ref, qkv_ref, out_ws, weights, normed_ref, dqkv_ref, bias_ref, small_ref, dn_ref, dm_ref,
    acc_ref,
):
    rows, cols = dm_ref.shape[0], weights[0].shape[2]
    heads = cols // HD
    for e, ow_ref in enumerate(out_ws):
        dm_ref[:, e * cols : (e + 1) * cols] = dot_nt(da_ref[...], ow_ref[...]).astype(BF16)

    @pl.loop(0, CORES * rows // (2 * seq))
    def _(step):
        lanes, pair = core_and_pair(step, rows // (2 * seq), cols)
        for i in (2 * pair, 2 * pair + 1):
            at = pl.ds(pl.multiple_of(i * seq, 16), seq)
            keys, vals = qkv_ref[1, at, lanes], qkv_ref[2, at, lanes]
            spread = spread_heads(qkv_ref[0, at, lanes], heads)
            probs = softmax_rows(spread, keys, vis_ref[pl.ds(i, 1), :])
            d_mixed = spread_heads(dm_ref[at, lanes], heads)
            d_probs = dot_nt(d_mixed, vals)
            inner = jnp.sum(probs * d_probs, axis=-1, keepdims=True)
            d_scores = (probs * (d_probs - inner)).astype(BF16)
            d_query = fold_heads(dot(d_scores, keys), heads)
            dqkv_ref[0, at, lanes] = (d_query * (HD**-0.5)).astype(BF16)
            dqkv_ref[1, at, lanes] = (dot_tn(d_scores, spread) * (HD**-0.5)).astype(BF16)
            dqkv_ref[2, at, lanes] = dot_tn(probs.astype(BF16), d_mixed).astype(BF16)

    acc_ref[...] = jnp.zeros_like(acc_ref)

    @pl.loop(0, 3)
    def _(t):
        for e, w_ref in enumerate(weights):
            acc_ref[...] += dot_nt(dqkv_ref[t, :, e * cols : (e + 1) * cols], w_ref[t])

    dn = acc_ref[...]
    dn_ref[...] = dn.astype(dn_ref.dtype)
    small_ref[0:1, :] = jnp.sum(dn * normed_ref[...].astype(F32), axis=0, keepdims=True)
    small_ref[1:2, :] = jnp.sum(dn, axis=0, keepdims=True)
    bias_ref[0:1, :] = jnp.sum(dqkv_ref[0].astype(F32), axis=0, keepdims=True)
    bias_ref[1:2, :] = jnp.sum(dqkv_ref[2].astype(F32), axis=0, keepdims=True)


def hidden_kernel(mixed, weights, tok_ref, bias_ref, gain_ref, shift_ref, hidden_ref, mid_ref):
    attn = None
    for m_ref, cores in zip(mixed, weights):
        size = m_ref.shape[1] // len(cores)
        for e, blocks in enumerate(cores):
            for i, w_ref in enumerate(blocks):
                part = w_ref.shape[0]
                at = e * size
                if len(blocks) > 1:
                    at = at + jnp.bitwise_xor(lax.axis_index("dp") & 1, i) * part
                    cut = m_ref[:, pl.ds(pl.multiple_of(at, part), part)]
                else:
                    cut = m_ref[:, at : at + part]
                term = dot(cut, w_ref[...])
                attn = term if attn is None else attn + term
    hidden = tok_ref[...].astype(F32) + (attn + bias_ref[...])
    hidden_ref[...] = hidden
    unit, _ = norm_stats(hidden)
    mid_ref[...] = (unit * gain_ref[...] + shift_ref[...]).astype(BF16)


def branch_kernel(dg_ref, dec_ref, db_ref):
    db_ref[...] = dot_nt(dg_ref[...], dec_ref[...]).astype(BF16)


def ffn_tile(mid, d_branch, fc1, b1, fc2):
    pre = dot(mid, fc1) + b1
    d_act = dot_nt(d_branch, fc2)
    cdf = 0.5 * (1.0 + lax.erf(pre * (0.5**0.5)))
    slope = cdf + pre * (jnp.exp(-0.5 * (pre * pre)) * 0.3989422804014327)
    return (pre * cdf).astype(BF16), (d_act * slope).astype(BF16)


def ffn_kernel(tile, mid_ref, db_ref, fc1_refs, b1_refs, fc2_refs, acts, d_pres, sums, out_ref, acc_ref):
    mid, branch = mid_ref[...], db_ref[...]
    acc_ref[...] = jnp.zeros_like(acc_ref)
    for e, (fc1_ref, b1_ref, fc2_ref) in enumerate(zip(fc1_refs, b1_refs, fc2_refs)):

        @pl.loop(0, fc1_ref.shape[1] // tile)
        def _(j):
            at = pl.ds(pl.multiple_of(j * tile, tile), tile)
            act, d_pre = ffn_tile(mid, branch, fc1_ref[:, at], b1_ref[:, at], fc2_ref[at, :])
            acts[e][:, at] = act
            d_pres[e][:, at] = d_pre
            sums[e][:, at] = jnp.sum(d_pre.astype(F32), axis=0, keepdims=True)
            acc_ref[...] += dot_nt(d_pre, fc1_ref[:, at])

    out_ref[...] = acc_ref[...].astype(out_ref.dtype)


def cut_cols(ref, axis, flips):
    width, at = ref.shape[1] // len(flips), lax.axis_index(axis)
    starts = [pl.multiple_of(jnp.bitwise_xor(at, flip) * width, width) for flip in flips]
    return jnp.concatenate([ref[:, pl.ds(start, width)] for start in starts], axis=1)


def overlaps(arrays, at, rows):
    first = 0
    for ref in arrays:
        low, high = max(at, first), min(at + rows, first + ref.shape[1])
        if low < high:
            yield ref, slice(low - first, high - first), slice(low - at, high - at)
        first += ref.shape[1]


def store_slices(total, got, outs, at):
    rows, width = total.shape[0], outs[0][0].shape[2]
    p = 0
    for group in outs:
        for k in range(group[0].shape[0]):
            piece = total[:, p * width : (p + 1) * width]
            if got:
                piece = piece + jnp.concatenate([ref[p, here].astype(F32) for ref, here, _ in overlaps(got, at, rows)])
            for ref, here, there in overlaps(group, at, rows):
                ref[k, here] = piece[there].astype(BF16)
            p += 1


def right_side(refs, flips):
    if flips:
        return jnp.concatenate([cut_cols(ref, "dp", flips) for ref in refs], axis=0)
    return jnp.concatenate([ref[...] for ref in refs], axis=0)


def ffn_grad_kernel(tile, flips, acts, d_pres, branches, mids, got, grads):
    left = jnp.concatenate([ref[:, tile] for ref in acts], axis=0)
    store_slices(dot_tn(left, right_side(branches, flips)), got, grads, 0)
    left = jnp.concatenate([ref[:, tile] for ref in d_pres], axis=0)
    store_slices(dot_tn(left, right_side(mids, flips)), got, grads, left.shape[1])


def grad_kernel(e, flips, takes, dqkvs, normed, mixed, d_attn, got, outs):
    at, cols = 0, dqkvs[0].shape[2] // CORES
    lanes = slice(e * cols, (e + 1) * cols)
    right = right_side(normed, flips)
    for t in takes:
        left = jnp.concatenate([ref[t, :, lanes] for ref in dqkvs], axis=0)
        store_slices(dot_tn(left, right), got, outs, at)
        at += cols
    if mixed:
        left = jnp.concatenate([ref[:, lanes] for ref in mixed], axis=0)
        store_slices(dot_tn(left, right_side(d_attn, flips)), got, outs, at)


def mlp_kernel(flips, fc2_refs, acts, hidden_ref, bias_ref, dgs, keep_ref, sends, dec_outs, low_ref):
    rows = keep_ref.shape[0]
    for d, cores in enumerate(acts):
        total = total_of([dot(ref[...], fc2_ref[...]) for ref, fc2_ref in zip(cores, fc2_refs)])
        if d == 0:
            keep_ref[...] = total
            total = total + (hidden_ref[...] + bias_ref[...])
        else:
            sends[d - 1][...] = total.astype(BF16)
        low_ref[d * rows : (d + 1) * rows] = total.astype(BF16)
    dg = jnp.concatenate([ref[...] for ref in dgs], axis=0)
    grads = dot_tn(cut_cols(low_ref, "mp", flips), dg)
    width, p = grads.shape[0] // len(flips), 0
    for out in dec_outs:
        for k in range(out.shape[0]):
            out[k] = grads[p * width : (p + 1) * width].astype(BF16)
            p += 1


def mid_back_kernel(keep_ref, far, hidden_ref, dg_ref, dec_ref, gain_ref, dh_ref, da_ref, small_ref):
    d_mid = total_of([keep_ref[...]] + [ref[...].astype(F32) for ref in far])
    unit, inv = norm_stats(hidden_ref[...])
    d_latent = dot_nt(dg_ref[...], dec_ref[...])
    d_hidden = d_latent + norm_back(unit, inv, gain_ref[...], d_mid)
    dh_ref[...] = d_hidden
    d_attn = d_hidden.astype(BF16)
    da_ref[...] = d_attn
    small_ref[0:1, :] = jnp.sum(d_mid * unit, axis=0, keepdims=True)
    small_ref[1:2, :] = jnp.sum(d_mid, axis=0, keepdims=True)
    small_ref[2:3, :] = jnp.sum(d_attn.astype(F32), axis=0, keepdims=True)
    small_ref[3:4, :] = jnp.sum(d_latent.astype(BF16).astype(F32), axis=0, keepdims=True)


def token_back_kernel(keep_ref, far, tok_ref, dh_ref, gain_ref, gt_ref):
    d_normed = total_of([keep_ref[...]] + [ref[...].astype(F32) for ref in far])
    unit, inv = norm_stats(tok_ref[...].astype(F32))
    gt_ref[...] = (dh_ref[...] + norm_back(unit, inv, gain_ref[...], d_normed)).astype(BF16)


def latent_kernel(keep_ref, far, hidden_ref, bias_ref, latent_ref):
    total = total_of([keep_ref[...]] + [ref[...].astype(F32) for ref in far])
    latent_ref[...] = (hidden_ref[...] + (total + bias_ref[...])).astype(BF16)


def plain_kernel(in_ref, out_ref):
    out_ref[...] = in_ref[...]


def stack_kernel(first_ref, second_ref, out_ref):
    half = first_ref.shape[0]
    out_ref[:half] = first_ref[...]
    out_ref[half:] = second_ref[...]


def place_kernel(axis, first_ref, second_ref, outs, all_ref):
    bits = (all_ref.shape[0] - 1).bit_length()
    half, size = first_ref.shape[0], first_ref.shape[1]
    all_ref[:half] = first_ref[...]
    all_ref[half:] = second_ref[...]
    owner = 0
    for out_ref in outs:
        for k in range(out_ref.shape[0] // size):
            flip = jnp.bitwise_xor(lax.axis_index(axis), owner)
            spot = sum(((flip >> i) & 1) << (bits - 1 - i) for i in range(bits))
            out_ref[k * size : (k + 1) * size] = all_ref[spot].astype(out_ref.dtype)
            owner += 1


def add_kernel(first_ref, second_ref, out_ref):
    out_ref[...] = (first_ref[...].astype(F32) + second_ref[...].astype(F32)).astype(out_ref.dtype)


def some_rows_kernel(first_ref, second_ref, out_ref):
    rows = second_ref.shape[0]
    out_ref[...] = first_ref[...]
    out_ref[:rows] = first_ref[:rows] + second_ref[...]


def small_kernel(small2_ref, normed_terms, fc1_terms, qv_terms, keep_ref, send_ref):
    for e, out_ref in enumerate((keep_ref, send_ref)):
        out_ref[...] = jnp.zeros_like(out_ref)
        out_ref[0:4, :] = small2_ref[...]
        out_ref[4:6, :] = total_of([ref[...] for ref in normed_terms])
        out_ref[6:7, : fc1_terms[e][0].shape[1]] = total_of([ref[...] for ref in fc1_terms[e]])
        total = total_of([ref[...] for ref in qv_terms])
        cols = total.shape[1] // CORES
        out_ref[7:8, :cols] = total[0:1, e * cols : (e + 1) * cols]
        out_ref[7:8, cols : 2 * cols] = total[1:2, e * cols : (e + 1) * cols]


def tick_kernel(out_ref):
    out_ref[...] = jnp.zeros_like(out_ref)


def fold_kernel(keep_ref, gots, low_ref, send_ref):
    half = low_ref.shape[0]
    for ref, here, there in overlaps(gots, 0, keep_ref.shape[1]):
        low_ref[:, there] = (keep_ref[:half, there].astype(F32) + ref[:half, here].astype(F32)).astype(BF16)
        send_ref[:, there] = (keep_ref[half:, there].astype(F32) + ref[half:, here].astype(F32)).astype(BF16)


def last_fold_kernel(pairs, lows, send_ref):
    for i, ((keep_ref, gots), low_ref) in enumerate(zip(pairs, lows)):
        fold_kernel(keep_ref, gots, low_ref, send_ref.at[pl.ds(i, 1)])


def finish_kernel(places, sums, outs):
    lows, gots = sums
    for i, (low_ref, pieces) in enumerate(zip(lows, places)):
        total = low_ref[0].astype(F32) + gots[i][i if gots[i].shape[0] > 1 else 0].astype(F32)
        size = total.shape[0] // len(pieces)
        for k, (which, flip, at) in enumerate(pieces):
            piece = total[k * size : (k + 1) * size]
            piece = piece.T if flip else piece
            if isinstance(at, int):
                outs[which][at] = piece
            elif at[0] is None:
                outs[which][:, at[1] : at[1] + piece.shape[1]] = piece
            else:
                outs[which][at[0] : at[0] + size] = piece


def put_exact(value, out_ref, at):
    rows, cols = value.shape[0], value.shape[1] // 2
    high = value.astype(BF16)
    low = (value - high.astype(F32)).astype(BF16)
    for i, part in enumerate((high[:, :cols], high[:, cols:], low[:, :cols], low[:, cols:])):
        out_ref[at + i * rows : at + (i + 1) * rows] = part


def get_exact(ref, at, rows):
    parts = [ref[at + i * rows : at + (i + 1) * rows].astype(F32) for i in range(4)]
    return jnp.concatenate([parts[0] + parts[2], parts[1] + parts[3]], axis=1)


def mix_kernel(keep_ref, got_ref, small_ref, out_ref):
    rows = keep_ref.shape[1]
    out_ref[:rows] = (keep_ref[0].astype(F32) + got_ref[0].astype(F32)).astype(BF16)
    put_exact(small_ref[...], out_ref, rows)


def mix_add_kernel(rows, first_ref, second_ref, out_ref):
    out_ref[:rows] = (first_ref[:rows].astype(F32) + second_ref[:rows].astype(F32)).astype(BF16)
    count = (out_ref.shape[0] - rows) // 4
    put_exact(get_exact(first_ref, rows, count) + get_exact(second_ref, rows, count), out_ref, rows)


def mix_end_kernel(rows, first_ref, second_ref, dec_ref, small_ref):
    dec_ref[0] = (first_ref[:rows].astype(F32) + second_ref[:rows].astype(F32)).astype(BF16)
    count = small_ref.shape[0]
    small_ref[...] = get_exact(first_ref, rows, count) + get_exact(second_ref, rows, count)


VMEM = pl.BlockSpec(memory_space=pltpu.VMEM)
ANY = pl.BlockSpec(memory_space=pl.ANY)


def like(shape, dtype=BF16):
    return jax.ShapeDtypeStruct(shape, dtype)


def nested_kernel(count, kernel, tree, *refs):
    kernel(*jax.tree.unflatten(tree, refs[count:]))


class Line:
    def __init__(self):
        self.last = []

    def __call__(self, kernel, outs, *args, after=(), limit=16, scratch=(), final=False):
        after = self.last + list(after)
        flat = jax.tree.leaves(args)
        out_flat, out_tree = jax.tree.flatten(outs)
        tree = jax.tree.structure((*args, *outs, *scratch))
        in_specs = [ANY] * len(after) + [VMEM] * len(flat)
        grid = {"grid": (1,)} if final else {}
        out_specs = [VMEM] * len(out_flat)
        if final:
            out_specs = [pl.BlockSpec(o.shape, lambda i, n=len(o.shape): (0,) * n) for o in out_flat]
        results = pl.pallas_call(
            functools.partial(nested_kernel, len(after), kernel, tree),
            out_shape=out_flat,
            in_specs=in_specs,
            out_specs=out_specs,
            scratch_shapes=list(scratch),
            compiler_params=pltpu.CompilerParams(vmem_limit_bytes=limit * MIB),
            cost_estimate=pl.CostEstimate(flops=1024, bytes_accessed=1024, transcendentals=0),
            **grid,
        )(*after, *flat)
        self.last = [min(results, key=lambda r: r.size)]
        return jax.tree.unflatten(out_tree, results)


class Moves:
    def __init__(self, n_mp, n_dp):
        self.n = {"mp": n_mp, "dp": n_dp}
        self.ny = n_mp // CORES

    def flip(self, value, axis, by):
        return lax.ppermute(value, axis, [(i, i ^ by) for i in range(self.n[axis])])

    def core(self, value):
        return self.flip(value, "mp", 1)

    def y(self, value, by, cross=0):
        pairs = [
            (y * CORES + c, ((y + by) % self.ny) * CORES + (c ^ cross))
            for y in range(self.ny)
            for c in range(CORES)
        ]
        return lax.ppermute(value, "mp", pairs)

    def bits(self, axis):
        return [1 << i for i in range((self.n[axis] - 1).bit_length())]

    def order(self, axis, bits=None):
        flips = [0]
        for bit in reversed(bits or self.bits(axis)):
            flips = flips + [f | bit for f in flips]
        return flips

    def total(self, value, axis, dtype):
        for bit in self.bits(axis):
            low = value.astype(dtype)
            value = low.astype(F32) + self.flip(low, axis, bit).astype(F32)
        return value


class Scatter:
    def __init__(self, line, moves, groups, bits, start=True):
        self.line, self.moves, self.bits = line, moves, list(bits)
        (self.keep,), self.held = groups
        if start:
            self.start(self.held)

    def start_after(self, value):
        first, *others = self.held
        *others, _ = lax.optimization_barrier((*others, value))
        self.start([first, *others])

    def start(self, sends):
        bit = self.bits.pop(0)
        self.got = [self.moves.flip(send, "dp", bit) for send in sends]

    def step(self):
        shape = like((self.keep.shape[0] // 2,) + self.keep.shape[1:])
        self.keep, send = self.line(fold_kernel, [shape, shape], self.keep, self.got)
        self.start([send])


def shards(
    tokens,
    visible,
    norm1_gain,
    norm1_shift,
    qkv_weight,
    qv_bias,
    out_weight,
    out_bias,
    norm2_gain,
    norm2_shift,
    fc1_weight,
    fc1_bias,
    fc2_weight,
    fc2_bias,
    dec_weight,
    decoded_grad,
):
    n_mp, n_dp = lax.axis_size("mp"), lax.axis_size("dp")
    moves, line = Moves(n_mp, n_dp), Line()
    ny = moves.ny
    rows, width = tokens.shape
    cols = qkv_weight.shape[2]
    units = fc1_weight.shape[1]
    dec = dec_weight.shape[1]
    images = visible.shape[0] // n_mp
    seq = rows // images
    mp_at, dp_at = lax.axis_index("mp"), lax.axis_index("dp")
    y_at, c_at = mp_at // CORES, mp_at % CORES
    row = lambda v: v.reshape(1, -1)
    gain1, shift1, gain2, shift2 = row(norm1_gain), row(norm1_shift), row(norm2_gain), row(norm2_shift)
    slice_cols = width // n_dp
    cuts = n_dp if slice_cols % 128 == 0 else 0
    dp_bits = moves.bits("dp")

    def dp_order(bits=None):
        return jnp.bitwise_xor(dp_at, jnp.array(moves.order("dp", bits), jnp.int32))

    def flips(bits=None):
        return moves.order("dp", bits) if cuts else []

    def grad_outs(rows_here, e, shares):
        split = lambda size, parts: [like((size, rows_here * part // sum(parts), slice_cols)) for part in parts]
        if cuts:
            return [split(n_dp, shares)] if e else [split(n_dp // 2, [1]), split(n_dp // 2, shares)]
        parts = shares if e else [1]
        return [[like((1, rows_here * part // sum(parts), width)) for part in parts]]

    def scatter(groups, bits, shares, start=True):
        if not cuts:
            natural = groups[0][0][0]
            slices = natural.reshape(-1, n_dp, slice_cols).transpose(1, 0, 2)[dp_order(bits)]
            ends, total = [sum(shares[: i + 1]) for i in range(len(shares) - 1)], sum(shares)
            ends = [slices.shape[1] * end // total for end in ends]
            groups = [slices[: n_dp // 2]], jnp.split(slices[n_dp // 2 :], ends, axis=1)
        return Scatter(line, moves, groups, bits, start)

    def last_steps(sums):
        for one in sums:
            while len(one.bits) > 1:
                one.step()
        bit = sums[0].bits[0]
        shape = (1,) + sums[0].keep.shape[1:]
        lows, send = line(
            last_fold_kernel, [[like(shape)] * len(sums), like((len(sums),) + shape[1:])],
            [(one.keep, one.got) for one in sums],
        )
        got = moves.flip(send, "dp", bit)
        return lows, [got] * len(sums)

    def finish(sums, shapes, spots):
        outs = [like(shape, F32) for shape in shapes]
        return line(functools.partial(finish_kernel, spots), [outs], sums, final=True)[0]

    counts = {}
    for d in range(ny):
        owner = lax.rem(y_at - d + ny, ny) * CORES + c_at
        own = lax.dynamic_slice_in_dim(visible, owner * images, images)
        counts[d] = jnp.broadcast_to(own[:, None], (images, 128))
    full, wide = like((rows, width)), like((rows, width), F32)
    far = list(reversed(range(1, ny)))

    def tick(*after):
        line(tick_kernel, [like((8, 128))], after=after)

    halved = (cols // 2) % 128 == 0 and n_dp > 1
    near = dp_at % 2
    out_part = lax.dynamic_slice_in_dim(out_weight, near * (cols // 2), cols // 2) if halved else out_weight
    out_w = {0: [[out_weight], [moves.core(out_weight)]]}
    for d in range(1, ny):
        pieces = [moves.y(out_part, d)]
        if halved:
            pieces.append(moves.flip(pieces[0], "dp", 1))
        out_w[d] = [pieces, [moves.core(v) for v in pieces]]
    tok, grad = {0: tokens}, {0: decoded_grad}
    for d in range(1, ny):
        tok[d] = moves.y(tokens, d)
    for d in range(1, ny):
        grad[d] = moves.y(decoded_grad, d)
    qkv_w = [qkv_weight, moves.core(qkv_weight)]
    bias_pair = jnp.concatenate([qv_bias.reshape(-1), fc1_bias])
    bias_other = moves.core(bias_pair)
    qv_b = [qv_bias, bias_other[: 2 * cols].reshape(2, cols)]
    b1 = [row(fc1_bias), row(bias_other[2 * cols :])]
    fc1_w = [fc1_weight, moves.core(fc1_weight)]
    fc2_w = [fc2_weight, moves.core(fc2_weight)]
    normed, qkv, mixed, d_branch = {}, {}, {}, {}

    def first_norm(d):
        (normed[d],) = line(norm_kernel, [full], tok[d], gain1, shift1)

    def branch(d):
        (d_branch[d],) = line(branch_kernel, [full], grad[d], dec_weight)

    def attend(d):
        qkv[d], mixed[d] = line(
            functools.partial(attn_fwd_kernel, seq),
            [like((3, rows, CORES * cols)), like((rows, CORES * cols))],
            counts[d], normed[d], qkv_w, qv_b,
        )

    gathered = {d: {} for d in range(ny)}

    def send_mixed(d):
        gathered[d][0] = mixed[d]
        for s in range(1, ny):
            gathered[(d + s) % ny][s] = moves.y(mixed[d], s)

    def settle(value):
        return line(plain_kernel, [like(value.shape)], value)[0]

    first_norm(0)
    qkv_w[1] = settle(qkv_w[1])
    attend(0)
    send_mixed(0)
    fc1_w[1] = settle(fc1_w[1])
    branch(0)
    fc2_w[1] = settle(fc2_w[1])
    for d in range(1, ny):
        first_norm(d)
        attend(d)
        send_mixed(d)

    hidden, mid = {}, {}

    def to_hidden(d):
        tick(*[gathered[d][s] for s in range(1, ny)])
        hidden[d], mid[d] = line(
            hidden_kernel, [wide, full],
            [gathered[d][s] for s in range(ny)], [out_w[s] for s in range(ny)],
            tok[d], row(out_bias), gain2, shift2,
        )

    act, d_pre, fc1_sums, dmid = {}, {}, {}, {}
    both, all_d = range(CORES), list(range(ny))

    def feed_forward(d):
        act[d], d_pre[d], fc1_sums[d], dmid[d] = line(
            functools.partial(ffn_kernel, min(512, units)),
            [[like((rows, units))] * CORES, [like((rows, units))] * CORES, [like((1, units), F32)] * CORES]
            + [full if d else wide],
            mid[d], d_branch[d], fc1_w, b1, fc2_w,
            scratch=[pltpu.VMEM((rows, width), F32)],
        )

    for d in far:
        to_hidden(d)
        branch(d)
        feed_forward(d)
        dmid[d] = moves.y(dmid[d], -d)
    to_hidden(0)
    feed_forward(0)

    tile = min(512, units)
    steps = units // tile
    swapped = dp_bits[1:2] + dp_bits[:1] + dp_bits[2:]
    tile_bits = [swapped if j % 2 else dp_bits for j in range(steps)]
    fc_sums, fc_got = [], {}

    def ffn_grads(e, j, shares):
        groups = line(
            functools.partial(ffn_grad_kernel, slice(j * tile, (j + 1) * tile), flips(tile_bits[j])),
            [grad_outs(2 * tile, e, shares)],
            [act[d][e] for d in all_d], [d_pre[d][e] for d in all_d],
            [d_branch[d] for d in all_d], [mid[d] for d in all_d], [] if e else fc_got[j],
        )[0]
        if e:
            fc_got[j] = [moves.core(v) for v in groups[0]]
        else:
            fc_sums.append(scatter(groups, tile_bits[j], shares))

    dec_bits = moves.bits("mp")
    dec_shape = like((n_mp // 2, width // n_mp, dec))
    mlp_keep, mlp_send, (dec_total, dec_send) = line(
        functools.partial(mlp_kernel, moves.order("mp")),
        [wide, [full] * (ny - 1), [dec_shape] * 2],
        fc2_w, [act[d] for d in all_d], hidden[0], row(fc2_bias), [grad[d] for d in all_d],
        limit=24, scratch=[pltpu.VMEM((ny * rows, width), BF16)],
    )
    dec_got = moves.flip(dec_send, "mp", dec_bits[0])

    d_hidden, d_attn_own, small2 = line(
        mid_back_kernel, [wide, full, like((4, width), F32)],
        dmid[0], [dmid[d] for d in range(1, ny)], hidden[0], decoded_grad, dec_weight, gain2,
    )
    d_attn = {0: d_attn_own}
    for s in range(1, ny):
        d_attn[s] = moves.y(d_attn_own, s)
    for bit in dec_bits[1:]:
        shape = like((dec_total.shape[0] // 2,) + dec_total.shape[1:])
        dec_total, dec_send = line(fold_kernel, [shape, shape], dec_total, [dec_got])
        if bit != dec_bits[-1]:
            dec_got = moves.flip(dec_send, "mp", bit)
    for e in (1, 0):
        for j in range(steps):
            ffn_grads(e, j, [1, 1])

    dqkv, dn, qv_terms, small_terms = {}, {}, {}, {}

    def attn_back(d, after=()):
        dqkv[d], qv_terms[d], small_terms[d], dn[d] = line(
            functools.partial(attn_bwd_kernel, seq),
            [like((3, rows, CORES * cols)), like((2, CORES * cols), F32), like((2, width), F32)]
            + [full if d else wide],
            counts[d], d_attn[d], qkv[d], [w[0] for w in out_w[0]], qkv_w, normed[d],
            scratch=[pltpu.VMEM((rows, CORES * cols), BF16), pltpu.VMEM((rows, width), F32)], after=after,
        )

    attn_back(0)
    held = lax.optimization_barrier((dec_send, dqkv[0]))
    dec_got = moves.flip(held[0], "mp", dec_bits[-1])
    for d in far:
        attn_back(d)

    def last_grads(e, shares, got=()):
        return line(
            functools.partial(grad_kernel, e, flips(), (0, 1, 2)), [grad_outs(4 * cols, e, shares)],
            [dqkv[d] for d in all_d], [normed[d] for d in all_d],
            [mixed[d] for d in all_d], [d_attn[d] for d in all_d], list(got),
        )[0]

    small, small_send = line(
        small_kernel, [like((8, width), F32)] * 2,
        small2, [small_terms[d] for d in all_d], [[fc1_sums[d][e] for d in all_d] for e in both],
        [qv_terms[d] for d in all_d], after=[dec_got],
    )
    got = moves.core(small_send)
    send = last_grads(1, [1])[0]
    (small,) = line(add_kernel, [like(small.shape, F32)], small, got)
    got = moves.flip(small[:6], "mp", moves.bits("mp")[1])
    fc_sums[0].step()
    (small,) = line(some_rows_kernel, [like(small.shape, F32)], small, got)
    for bit in moves.bits("mp")[2:]:
        got = moves.flip(small[:6], "mp", bit)
        (small,) = line(some_rows_kernel, [like(small.shape, F32)], small, got)
    dec_rows = dec_total.shape[1]
    (mix,) = line(mix_kernel, [like((dec_rows + 4 * small.shape[0], dec))], dec_total, dec_got, small)
    mix_todo = dp_bits[::-1]
    mix_got = moves.flip(mix, "dp", mix_todo.pop(0))

    def mix_step():
        nonlocal mix, mix_got
        (mix,) = line(functools.partial(mix_add_kernel, dec_rows), [like(mix.shape)], mix, mix_got)
        mix_got = moves.flip(mix, "dp", mix_todo.pop(0))

    for s in fc_sums[1:]:
        s.step()
    *held, _ = lax.optimization_barrier((*send, fc_sums[-1].keep))
    crossed = [moves.core(v) for v in held]
    for d in range(1, ny):
        (send,) = line(plain_kernel, [full], dn[d])
        dn[d] = moves.y(send, -d)
    last_sum = scatter(last_grads(0, [5, 3], crossed), dp_bits, [5, 3], start=False)
    last_fc = last_steps(fc_sums)
    mix_step()
    last_sum.start_after(mix)
    terms = [dn[d] for d in range(1, ny)]
    (grad_tokens,) = line(token_back_kernel, [full], dn[0], terms, tokens, d_hidden, gain1, final=True)
    while mix_todo:
        mix_step()
    last_sum.step()
    dec_total, small = line(
        functools.partial(mix_end_kernel, dec_rows), [like((1, dec_rows, dec)), like(small.shape, F32)], mix, mix_got
    )
    fc1_grad, fc2_grad = finish(
        last_fc,
        [(slice_cols, units), (units, slice_cols)],
        [[(1, False, (j * tile, None)), (0, True, (None, j * tile))] for j in range(steps)],
    )
    mlp_far = []
    for d in range(1, ny):
        (send,) = line(plain_kernel, [full], mlp_send[d - 1])
        mlp_far.append(moves.y(send, -d))
    dec_bits_back = list(reversed(dec_bits))
    for bit in dec_bits_back[:-1]:
        dec_got = moves.flip(dec_total, "mp", bit)
        shape = (2 * dec_total.shape[0],) + dec_total.shape[1:]
        (dec_total,) = line(stack_kernel, [like(shape)], dec_total, dec_got)
    dec_got = moves.flip(dec_total, "mp", dec_bits_back[-1])
    while last_sum.bits:
        last_sum.step()
    (grad_dec_weight,) = line(
        functools.partial(place_kernel, "mp"), [[like((width, dec), F32)]], dec_total, dec_got, final=True,
        scratch=[pltpu.VMEM((n_mp, width // n_mp, dec), BF16)],
    )[0]
    (latent,) = line(latent_kernel, [full], mlp_keep, mlp_far, hidden[0], row(fc2_bias), final=True)
    norm1_shift_grad = small[5]
    norm1_gain_grad = (small[4] - norm1_shift * norm1_shift_grad) / norm1_gain
    grad_qv_bias = small[7, : 2 * cols].reshape(2, cols)
    grad_qkv_weight, grad_out_weight = finish(
        ([last_sum.keep], last_sum.got),
        [(3, slice_cols, cols), (cols, slice_cols)],
        [[(0, True, 0), (0, True, 1), (0, True, 2), (1, False, (0, None))]],
    )
    return (
        latent,
        grad_tokens,
        norm1_gain_grad,
        norm1_shift_grad,
        grad_qkv_weight,
        grad_qv_bias,
        grad_out_weight,
        small[2],
        small[0],
        small[1],
        fc1_grad,
        small[6, :units],
        fc2_grad,
        small[3],
        grad_dec_weight,
    )


def solution(mesh):
    return jax.shard_map(
        shards,
        mesh=mesh,
        in_specs=(
            P(("dp", "mp"), None),
            P("dp"),
            P(),
            P(),
            P(None, None, "mp"),
            P(None, "mp"),
            P("mp", None),
            P(),
            P(),
            P(),
            P(None, "mp"),
            P("mp"),
            P("mp", None),
            P(),
            P(),
            P(("dp", "mp"), None),
        ),
        out_specs=(
            P(("dp", "mp"), None),
            P(("dp", "mp"), None),
            P(),
            P(),
            P(None, "dp", "mp"),
            P(None, "mp"),
            P("mp", "dp"),
            P(),
            P(),
            P(),
            P("dp", "mp"),
            P("mp"),
            P("mp", "dp"),
            P(),
            P(),
        ),
        check_vma=False,
    )
```

```python
import functools

import jax
import jax.numpy as jnp
from jax import lax
from jax.experimental import pallas as pl
from jax.experimental.pallas import tpu as pltpu
from jax.sharding import PartitionSpec as P

HD = 64
CORES = 2
EPS = 1e-06
F32 = jnp.float32
BF16 = jnp.bfloat16
MIB = 1 << 20


def dot(lhs, rhs):
    return jnp.dot(lhs, rhs, preferred_element_type=F32)


def dot_nt(lhs, rhs):
    return lax.dot_general(lhs, rhs, (((1,), (1,)), ((), ())), preferred_element_type=F32)


def dot_tn(lhs, rhs):
    return lax.dot_general(lhs, rhs, (((0,), (0,)), ((), ())), preferred_element_type=F32)


def total_of(terms):
    return functools.reduce(jnp.add, terms)


def norm_stats(values):
    row_mean = jnp.mean(values, axis=-1, keepdims=True)
    centered = values - row_mean
    variance = jnp.mean(centered * centered, axis=-1, keepdims=True)
    inv = lax.rsqrt(variance + EPS)
    return centered * inv, inv


def norm_back(unit, inv, gain, grad):
    scaled = grad * gain
    first = jnp.mean(scaled, axis=-1, keepdims=True)
    second = jnp.mean(scaled * unit, axis=-1, keepdims=True)
    return inv * (scaled - first - unit * second)


def head_mask(cols, head, dtype):
    lane = lax.broadcasted_iota(jnp.int32, (1, cols), 1)
    return jnp.where((lane >= head * HD) & (lane < (head + 1) * HD), 1.0, 0.0).astype(dtype)


def spread_heads(rows, heads):
    cols = rows.shape[1]
    return jnp.concatenate([rows * head_mask(cols, h, rows.dtype) for h in range(heads)], axis=0)


def fold_heads(stacked, heads):
    seq, cols = stacked.shape[0] // heads, stacked.shape[1]
    total = stacked[:seq] * head_mask(cols, 0, stacked.dtype)
    for h in range(1, heads):
        total = total + stacked[h * seq : (h + 1) * seq] * head_mask(cols, h, stacked.dtype)
    return total


def softmax_rows(spread, keys, count):
    scores = dot_nt(spread, keys) * (HD**-0.5)
    col = lax.broadcasted_iota(jnp.int32, scores.shape, 1)
    scores = jnp.where(col <= count[:, : scores.shape[1]], scores, -1e30)
    top = jnp.max(scores, axis=-1, keepdims=True)
    exps = jnp.exp(scores - top)
    return exps / jnp.sum(exps, axis=-1, keepdims=True)


def norm_kernel(tok_ref, gain_ref, shift_ref, normed_ref):
    unit, _ = norm_stats(tok_ref[...].astype(F32))
    normed_ref[...] = (unit * gain_ref[...] + shift_ref[...]).astype(BF16)


def attn_fwd_kernel(seq, vis_ref, normed_ref, weights, biases, qkv_ref, mixed_ref):
    normed = normed_ref[...]
    rows, cols = normed.shape[0], weights[0].shape[2]
    heads = cols // HD
    for e, (w_ref, b_ref) in enumerate(zip(weights, biases)):
        lanes = slice(e * cols, (e + 1) * cols)
        for t, bias in ((0, 0), (1, None), (2, 1)):
            part = dot(normed, w_ref[t])
            if bias is not None:
                part = part + b_ref[bias : bias + 1, :]
            qkv_ref[t, :, lanes] = part.astype(BF16)

    @pl.loop(0, CORES * rows // (2 * seq))
    def _(step):
        lanes, pair = core_and_pair(step, rows // (2 * seq), cols)
        for i in (2 * pair, 2 * pair + 1):
            at = pl.ds(pl.multiple_of(i * seq, 16), seq)
            spread = spread_heads(qkv_ref[0, at, lanes], heads)
            probs = softmax_rows(spread, qkv_ref[1, at, lanes], vis_ref[pl.ds(i, 1), :])
            out = dot(probs.astype(BF16), qkv_ref[2, at, lanes])
            mixed_ref[at, lanes] = fold_heads(out, heads).astype(BF16)


def core_and_pair(step, pairs, cols):
    core = step // pairs
    return pl.ds(pl.multiple_of(core * cols, cols), cols), step - core * pairs


def attn_bwd_kernel(
    seq, vis_ref, da_ref, qkv_ref, out_ws, weights, normed_ref, dqkv_ref, bias_ref, small_ref, dn_ref, dm_ref,
    acc_ref,
):
    rows, cols = dm_ref.shape[0], weights[0].shape[2]
    heads = cols // HD
    for e, ow_ref in enumerate(out_ws):
        dm_ref[:, e * cols : (e + 1) * cols] = dot_nt(da_ref[...], ow_ref[...]).astype(BF16)

    @pl.loop(0, CORES * rows // (2 * seq))
    def _(step):
        lanes, pair = core_and_pair(step, rows // (2 * seq), cols)
        for i in (2 * pair, 2 * pair + 1):
            at = pl.ds(pl.multiple_of(i * seq, 16), seq)
            keys, vals = qkv_ref[1, at, lanes], qkv_ref[2, at, lanes]
            spread = spread_heads(qkv_ref[0, at, lanes], heads)
            probs = softmax_rows(spread, keys, vis_ref[pl.ds(i, 1), :])
            d_mixed = spread_heads(dm_ref[at, lanes], heads)
            d_probs = dot_nt(d_mixed, vals)
            inner = jnp.sum(probs * d_probs, axis=-1, keepdims=True)
            d_scores = (probs * (d_probs - inner)).astype(BF16)
            d_query = fold_heads(dot(d_scores, keys), heads)
            dqkv_ref[0, at, lanes] = (d_query * (HD**-0.5)).astype(BF16)
            dqkv_ref[1, at, lanes] = (dot_tn(d_scores, spread) * (HD**-0.5)).astype(BF16)
            dqkv_ref[2, at, lanes] = dot_tn(probs.astype(BF16), d_mixed).astype(BF16)

    acc_ref[...] = jnp.zeros_like(acc_ref)

    @pl.loop(0, 3)
    def _(t):
        for e, w_ref in enumerate(weights):
            acc_ref[...] += dot_nt(dqkv_ref[t, :, e * cols : (e + 1) * cols], w_ref[t])

    dn = acc_ref[...]
    dn_ref[...] = dn.astype(dn_ref.dtype)
    small_ref[0:1, :] = jnp.sum(dn * normed_ref[...].astype(F32), axis=0, keepdims=True)
    small_ref[1:2, :] = jnp.sum(dn, axis=0, keepdims=True)
    bias_ref[0:1, :] = jnp.sum(dqkv_ref[0].astype(F32), axis=0, keepdims=True)
    bias_ref[1:2, :] = jnp.sum(dqkv_ref[2].astype(F32), axis=0, keepdims=True)


def hidden_kernel(mixed, weights, tok_ref, bias_ref, gain_ref, shift_ref, hidden_ref, mid_ref):
    attn = None
    for m_ref, cores in zip(mixed, weights):
        size = m_ref.shape[1] // len(cores)
        for e, blocks in enumerate(cores):
            for i, w_ref in enumerate(blocks):
                part = w_ref.shape[0]
                at = e * size
                if len(blocks) > 1:
                    at = at + jnp.bitwise_xor(lax.axis_index("dp") & 1, i) * part
                    cut = m_ref[:, pl.ds(pl.multiple_of(at, part), part)]
                else:
                    cut = m_ref[:, at : at + part]
                term = dot(cut, w_ref[...])
                attn = term if attn is None else attn + term
    hidden = tok_ref[...].astype(F32) + (attn + bias_ref[...])
    hidden_ref[...] = hidden
    unit, _ = norm_stats(hidden)
    mid_ref[...] = (unit * gain_ref[...] + shift_ref[...]).astype(BF16)


def branch_kernel(dg_ref, dec_ref, db_ref):
    db_ref[...] = dot_nt(dg_ref[...], dec_ref[...]).astype(BF16)


def ffn_tile(mid, d_branch, fc1, b1, fc2):
    pre = dot(mid, fc1) + b1
    d_act = dot_nt(d_branch, fc2)
    cdf = 0.5 * (1.0 + lax.erf(pre * (0.5**0.5)))
    slope = cdf + pre * (jnp.exp(-0.5 * (pre * pre)) * 0.3989422804014327)
    return (pre * cdf).astype(BF16), (d_act * slope).astype(BF16)


def ffn_kernel(tile, mid_ref, db_ref, fc1_refs, b1_refs, fc2_refs, acts, d_pres, sums, out_ref, acc_ref):
    mid, branch = mid_ref[...], db_ref[...]
    acc_ref[...] = jnp.zeros_like(acc_ref)
    for e, (fc1_ref, b1_ref, fc2_ref) in enumerate(zip(fc1_refs, b1_refs, fc2_refs)):

        @pl.loop(0, fc1_ref.shape[1] // tile)
        def _(j):
            at = pl.ds(pl.multiple_of(j * tile, tile), tile)
            act, d_pre = ffn_tile(mid, branch, fc1_ref[:, at], b1_ref[:, at], fc2_ref[at, :])
            acts[e][:, at] = act
            d_pres[e][:, at] = d_pre
            sums[e][:, at] = jnp.sum(d_pre.astype(F32), axis=0, keepdims=True)
            acc_ref[...] += dot_nt(d_pre, fc1_ref[:, at])

    out_ref[...] = acc_ref[...].astype(out_ref.dtype)


def cut_cols(ref, axis, flips):
    width, at = ref.shape[1] // len(flips), lax.axis_index(axis)
    starts = [pl.multiple_of(jnp.bitwise_xor(at, flip) * width, width) for flip in flips]
    return jnp.concatenate([ref[:, pl.ds(start, width)] for start in starts], axis=1)


def overlaps(arrays, at, rows):
    first = 0
    for ref in arrays:
        low, high = max(at, first), min(at + rows, first + ref.shape[1])
        if low < high:
            yield ref, slice(low - first, high - first), slice(low - at, high - at)
        first += ref.shape[1]


def store_slices(total, got, outs, at):
    rows, width = total.shape[0], outs[0][0].shape[2]
    p = 0
    for group in outs:
        for k in range(group[0].shape[0]):
            piece = total[:, p * width : (p + 1) * width]
            if got:
                piece = piece + jnp.concatenate([ref[p, here].astype(F32) for ref, here, _ in overlaps(got, at, rows)])
            for ref, here, there in overlaps(group, at, rows):
                ref[k, here] = piece[there].astype(BF16)
            p += 1


def right_side(refs, flips):
    if flips:
        return jnp.concatenate([cut_cols(ref, "dp", flips) for ref in refs], axis=0)
    return jnp.concatenate([ref[...] for ref in refs], axis=0)


def ffn_grad_kernel(tile, flips, acts, d_pres, branches, mids, got, grads):
    left = jnp.concatenate([ref[:, tile] for ref in acts], axis=0)
    store_slices(dot_tn(left, right_side(branches, flips)), got, grads, 0)
    left = jnp.concatenate([ref[:, tile] for ref in d_pres], axis=0)
    store_slices(dot_tn(left, right_side(mids, flips)), got, grads, left.shape[1])


def grad_kernel(e, flips, takes, dqkvs, normed, mixed, d_attn, got, outs):
    at, cols = 0, dqkvs[0].shape[2] // CORES
    lanes = slice(e * cols, (e + 1) * cols)
    right = right_side(normed, flips)
    for t in takes:
        left = jnp.concatenate([ref[t, :, lanes] for ref in dqkvs], axis=0)
        store_slices(dot_tn(left, right), got, outs, at)
        at += cols
    if mixed:
        left = jnp.concatenate([ref[:, lanes] for ref in mixed], axis=0)
        store_slices(dot_tn(left, right_side(d_attn, flips)), got, outs, at)


def mlp_kernel(flips, fc2_refs, acts, hidden_ref, bias_ref, dgs, keep_ref, sends, dec_outs, low_ref):
    rows = keep_ref.shape[0]
    for d, cores in enumerate(acts):
        total = total_of([dot(ref[...], fc2_ref[...]) for ref, fc2_ref in zip(cores, fc2_refs)])
        if d == 0:
            total = total + (hidden_ref[...] + bias_ref[...])
            keep_ref[...] = total
        else:
            sends[d - 1][...] = total.astype(BF16)
        low_ref[d * rows : (d + 1) * rows] = total.astype(BF16)
    dg = jnp.concatenate([ref[...] for ref in dgs], axis=0)
    grads = dot_tn(cut_cols(low_ref, "mp", flips), dg)
    width, p = grads.shape[0] // len(flips), 0
    for out in dec_outs:
        for k in range(out.shape[0]):
            out[k] = grads[p * width : (p + 1) * width].astype(BF16)
            p += 1


def mid_back_kernel(keep_ref, far, hidden_ref, dg_ref, dec_ref, gain_ref, dh_ref, da_ref, small_ref):
    d_mid = total_of([keep_ref[...]] + [ref[...].astype(F32) for ref in far])
    unit, inv = norm_stats(hidden_ref[...])
    d_latent = dot_nt(dg_ref[...], dec_ref[...])
    d_hidden = d_latent + norm_back(unit, inv, gain_ref[...], d_mid)
    dh_ref[...] = d_hidden
    d_attn = d_hidden.astype(BF16)
    da_ref[...] = d_attn
    small_ref[0:1, :] = jnp.sum(d_mid * unit, axis=0, keepdims=True)
    small_ref[1:2, :] = jnp.sum(d_mid, axis=0, keepdims=True)
    small_ref[2:3, :] = jnp.sum(d_attn.astype(F32), axis=0, keepdims=True)
    small_ref[3:4, :] = jnp.sum(d_latent.astype(BF16).astype(F32), axis=0, keepdims=True)


def token_back_kernel(keep_ref, far, tok_ref, dh_ref, gain_ref, gt_ref):
    d_normed = total_of([keep_ref[...]] + [ref[...].astype(F32) for ref in far])
    unit, inv = norm_stats(tok_ref[...].astype(F32))
    gt_ref[...] = (dh_ref[...] + norm_back(unit, inv, gain_ref[...], d_normed)).astype(BF16)


def latent_kernel(keep_ref, far, latent_ref):
    latent_ref[...] = total_of([keep_ref[...]] + [ref[...].astype(F32) for ref in far]).astype(BF16)


def plain_kernel(in_ref, out_ref):
    out_ref[...] = in_ref[...]


def stack_kernel(first_ref, second_ref, out_ref):
    half = first_ref.shape[0]
    out_ref[:half] = first_ref[...]
    out_ref[half:] = second_ref[...]


def place_kernel(axis, first_ref, second_ref, outs, all_ref):
    bits = (all_ref.shape[0] - 1).bit_length()
    half, size = first_ref.shape[0], first_ref.shape[1]
    all_ref[:half] = first_ref[...]
    all_ref[half:] = second_ref[...]
    owner = 0
    for out_ref in outs:
        for k in range(out_ref.shape[0] // size):
            flip = jnp.bitwise_xor(lax.axis_index(axis), owner)
            spot = sum(((flip >> i) & 1) << (bits - 1 - i) for i in range(bits))
            out_ref[k * size : (k + 1) * size] = all_ref[spot].astype(out_ref.dtype)
            owner += 1


def add_kernel(first_ref, second_ref, out_ref):
    out_ref[...] = (first_ref[...].astype(F32) + second_ref[...].astype(F32)).astype(out_ref.dtype)


def some_rows_kernel(first_ref, second_ref, out_ref):
    rows = second_ref.shape[0]
    out_ref[...] = first_ref[...]
    out_ref[:rows] = first_ref[:rows] + second_ref[...]


def small_kernel(small2_ref, normed_terms, fc1_terms, qv_terms, keep_ref, send_ref):
    for e, out_ref in enumerate((keep_ref, send_ref)):
        out_ref[...] = jnp.zeros_like(out_ref)
        out_ref[0:4, :] = small2_ref[...]
        out_ref[4:6, :] = total_of([ref[...] for ref in normed_terms])
        out_ref[6:7, : fc1_terms[e][0].shape[1]] = total_of([ref[...] for ref in fc1_terms[e]])
        total = total_of([ref[...] for ref in qv_terms])
        cols = total.shape[1] // CORES
        out_ref[7:8, :cols] = total[0:1, e * cols : (e + 1) * cols]
        out_ref[7:8, cols : 2 * cols] = total[1:2, e * cols : (e + 1) * cols]


def tick_kernel(out_ref):
    out_ref[...] = jnp.zeros_like(out_ref)


def fold_kernel(keep_ref, gots, low_ref, send_ref):
    half = low_ref.shape[0]
    for ref, here, there in overlaps(gots, 0, keep_ref.shape[1]):
        low_ref[:, there] = (keep_ref[:half, there].astype(F32) + ref[:half, here].astype(F32)).astype(BF16)
        send_ref[:, there] = (keep_ref[half:, there].astype(F32) + ref[half:, here].astype(F32)).astype(BF16)


def last_fold_kernel(pairs, lows, send_ref):
    for i, ((keep_ref, gots), low_ref) in enumerate(zip(pairs, lows)):
        fold_kernel(keep_ref, gots, low_ref, send_ref.at[pl.ds(i, 1)])


def finish_kernel(places, sums, outs):
    lows, gots = sums
    for i, (low_ref, pieces) in enumerate(zip(lows, places)):
        total = low_ref[0].astype(F32) + gots[i][i if gots[i].shape[0] > 1 else 0].astype(F32)
        size = total.shape[0] // len(pieces)
        for k, (which, flip, at) in enumerate(pieces):
            piece = total[k * size : (k + 1) * size]
            piece = piece.T if flip else piece
            if isinstance(at, int):
                outs[which][at] = piece
            elif at[0] is None:
                outs[which][:, at[1] : at[1] + piece.shape[1]] = piece
            else:
                outs[which][at[0] : at[0] + size] = piece


def put_exact(value, out_ref, at):
    rows, cols = value.shape[0], value.shape[1] // 2
    high = value.astype(BF16)
    low = (value - high.astype(F32)).astype(BF16)
    for i, part in enumerate((high[:, :cols], high[:, cols:], low[:, :cols], low[:, cols:])):
        out_ref[at + i * rows : at + (i + 1) * rows] = part


def get_exact(ref, at, rows):
    parts = [ref[at + i * rows : at + (i + 1) * rows].astype(F32) for i in range(4)]
    return jnp.concatenate([parts[0] + parts[2], parts[1] + parts[3]], axis=1)


def mix_kernel(keep_ref, got_ref, small_ref, out_ref):
    rows = keep_ref.shape[1]
    out_ref[:rows] = (keep_ref[0].astype(F32) + got_ref[0].astype(F32)).astype(BF16)
    put_exact(small_ref[...], out_ref, rows)


def mix_add_kernel(rows, first_ref, second_ref, out_ref):
    out_ref[:rows] = (first_ref[:rows].astype(F32) + second_ref[:rows].astype(F32)).astype(BF16)
    count = (out_ref.shape[0] - rows) // 4
    put_exact(get_exact(first_ref, rows, count) + get_exact(second_ref, rows, count), out_ref, rows)


def mix_end_kernel(rows, first_ref, second_ref, dec_ref, small_ref):
    dec_ref[0] = (first_ref[:rows].astype(F32) + second_ref[:rows].astype(F32)).astype(BF16)
    count = small_ref.shape[0]
    small_ref[...] = get_exact(first_ref, rows, count) + get_exact(second_ref, rows, count)


VMEM = pl.BlockSpec(memory_space=pltpu.VMEM)
ANY = pl.BlockSpec(memory_space=pl.ANY)


def like(shape, dtype=BF16):
    return jax.ShapeDtypeStruct(shape, dtype)


def nested_kernel(count, kernel, tree, *refs):
    kernel(*jax.tree.unflatten(tree, refs[count:]))


class Line:
    def __init__(self):
        self.last = []

    def __call__(self, kernel, outs, *args, after=(), limit=16, scratch=(), final=False):
        after = self.last + list(after)
        flat = jax.tree.leaves(args)
        out_flat, out_tree = jax.tree.flatten(outs)
        tree = jax.tree.structure((*args, *outs, *scratch))
        in_specs = [ANY] * len(after) + [VMEM] * len(flat)
        grid = {"grid": (1,)} if final else {}
        out_specs = [VMEM] * len(out_flat)
        if final:
            out_specs = [pl.BlockSpec(o.shape, lambda i, n=len(o.shape): (0,) * n) for o in out_flat]
        results = pl.pallas_call(
            functools.partial(nested_kernel, len(after), kernel, tree),
            out_shape=out_flat,
            in_specs=in_specs,
            out_specs=out_specs,
            scratch_shapes=list(scratch),
            compiler_params=pltpu.CompilerParams(vmem_limit_bytes=limit * MIB),
            cost_estimate=pl.CostEstimate(flops=1024, bytes_accessed=1024, transcendentals=0),
            **grid,
        )(*after, *flat)
        self.last = [min(results, key=lambda r: r.size)]
        return jax.tree.unflatten(out_tree, results)


class Moves:
    def __init__(self, n_mp, n_dp):
        self.n = {"mp": n_mp, "dp": n_dp}
        self.ny = n_mp // CORES

    def flip(self, value, axis, by):
        return lax.ppermute(value, axis, [(i, i ^ by) for i in range(self.n[axis])])

    def core(self, value):
        return self.flip(value, "mp", 1)

    def y(self, value, by, cross=0):
        pairs = [
            (y * CORES + c, ((y + by) % self.ny) * CORES + (c ^ cross))
            for y in range(self.ny)
            for c in range(CORES)
        ]
        return lax.ppermute(value, "mp", pairs)

    def bits(self, axis):
        return [1 << i for i in range((self.n[axis] - 1).bit_length())]

    def order(self, axis, bits=None):
        flips = [0]
        for bit in reversed(bits or self.bits(axis)):
            flips = flips + [f | bit for f in flips]
        return flips

    def total(self, value, axis, dtype):
        for bit in self.bits(axis):
            low = value.astype(dtype)
            value = low.astype(F32) + self.flip(low, axis, bit).astype(F32)
        return value


class Scatter:
    def __init__(self, line, moves, groups, bits, start=True):
        self.line, self.moves, self.bits = line, moves, list(bits)
        (self.keep,), self.held = groups
        if start:
            self.start(self.held)

    def start_after(self, value):
        first, *others = self.held
        *others, _ = lax.optimization_barrier((*others, value))
        self.start([first, *others])

    def start(self, sends):
        bit = self.bits.pop(0)
        self.got = [self.moves.flip(send, "dp", bit) for send in sends]

    def step(self):
        shape = like((self.keep.shape[0] // 2,) + self.keep.shape[1:])
        self.keep, send = self.line(fold_kernel, [shape, shape], self.keep, self.got)
        self.start([send])


def shards(
    tokens,
    visible,
    norm1_gain,
    norm1_shift,
    qkv_weight,
    qv_bias,
    out_weight,
    out_bias,
    norm2_gain,
    norm2_shift,
    fc1_weight,
    fc1_bias,
    fc2_weight,
    fc2_bias,
    dec_weight,
    decoded_grad,
):
    n_mp, n_dp = lax.axis_size("mp"), lax.axis_size("dp")
    moves, line = Moves(n_mp, n_dp), Line()
    ny = moves.ny
    rows, width = tokens.shape
    cols = qkv_weight.shape[2]
    units = fc1_weight.shape[1]
    dec = dec_weight.shape[1]
    images = visible.shape[0] // n_mp
    seq = rows // images
    mp_at, dp_at = lax.axis_index("mp"), lax.axis_index("dp")
    y_at, c_at = mp_at // CORES, mp_at % CORES
    row = lambda v: v.reshape(1, -1)
    gain1, shift1, gain2, shift2 = row(norm1_gain), row(norm1_shift), row(norm2_gain), row(norm2_shift)
    slice_cols = width // n_dp
    cuts = n_dp if slice_cols % 128 == 0 else 0
    dp_bits = moves.bits("dp")

    def dp_order(bits=None):
        return jnp.bitwise_xor(dp_at, jnp.array(moves.order("dp", bits), jnp.int32))

    def flips(bits=None):
        return moves.order("dp", bits) if cuts else []

    def grad_outs(rows_here, e, shares):
        split = lambda size, parts: [like((size, rows_here * part // sum(parts), slice_cols)) for part in parts]
        if cuts:
            return [split(n_dp, shares)] if e else [split(n_dp // 2, [1]), split(n_dp // 2, shares)]
        parts = shares if e else [1]
        return [[like((1, rows_here * part // sum(parts), width)) for part in parts]]

    def scatter(groups, bits, shares, start=True):
        if not cuts:
            natural = groups[0][0][0]
            slices = natural.reshape(-1, n_dp, slice_cols).transpose(1, 0, 2)[dp_order(bits)]
            ends, total = [sum(shares[: i + 1]) for i in range(len(shares) - 1)], sum(shares)
            ends = [slices.shape[1] * end // total for end in ends]
            groups = [slices[: n_dp // 2]], jnp.split(slices[n_dp // 2 :], ends, axis=1)
        return Scatter(line, moves, groups, bits, start)

    def last_steps(sums):
        for one in sums:
            while len(one.bits) > 1:
                one.step()
        bit = sums[0].bits[0]
        shape = (1,) + sums[0].keep.shape[1:]
        lows, send = line(
            last_fold_kernel, [[like(shape)] * len(sums), like((len(sums),) + shape[1:])],
            [(one.keep, one.got) for one in sums],
        )
        got = moves.flip(send, "dp", bit)
        return lows, [got] * len(sums)

    def finish(sums, shapes, spots):
        outs = [like(shape, F32) for shape in shapes]
        return line(functools.partial(finish_kernel, spots), [outs], sums, final=True)[0]

    counts = {}
    for d in range(ny):
        owner = lax.rem(y_at - d + ny, ny) * CORES + c_at
        own = lax.dynamic_slice_in_dim(visible, owner * images, images)
        counts[d] = jnp.broadcast_to(own[:, None], (images, 128))
    full, wide = like((rows, width)), like((rows, width), F32)
    far = list(reversed(range(1, ny)))

    def tick(*after):
        line(tick_kernel, [like((8, 128))], after=after)

    halved = (cols // 2) % 128 == 0 and n_dp > 1
    near = dp_at % 2
    out_part = lax.dynamic_slice_in_dim(out_weight, near * (cols // 2), cols // 2) if halved else out_weight
    out_w = {0: [[out_weight], [moves.core(out_weight)]]}
    for d in range(1, ny):
        pieces = [moves.y(out_part, d)]
        if halved:
            pieces.append(moves.flip(pieces[0], "dp", 1))
        out_w[d] = [pieces, [moves.core(v) for v in pieces]]
    tok, grad = {0: tokens}, {0: decoded_grad}
    for d in range(1, ny):
        tok[d] = moves.y(tokens, d)
    for d in range(1, ny):
        grad[d] = moves.y(decoded_grad, d)
    qkv_w = [qkv_weight, moves.core(qkv_weight)]
    bias_pair = jnp.concatenate([qv_bias.reshape(-1), fc1_bias])
    bias_other = moves.core(bias_pair)
    qv_b = [qv_bias, bias_other[: 2 * cols].reshape(2, cols)]
    b1 = [row(fc1_bias), row(bias_other[2 * cols :])]
    fc1_w = [fc1_weight, moves.core(fc1_weight)]
    fc2_w = [fc2_weight, moves.core(fc2_weight)]
    normed, qkv, mixed, d_branch = {}, {}, {}, {}

    def first_norm(d):
        (normed[d],) = line(norm_kernel, [full], tok[d], gain1, shift1)

    def branch(d):
        (d_branch[d],) = line(branch_kernel, [full], grad[d], dec_weight)

    def attend(d):
        qkv[d], mixed[d] = line(
            functools.partial(attn_fwd_kernel, seq),
            [like((3, rows, CORES * cols)), like((rows, CORES * cols))],
            counts[d], normed[d], qkv_w, qv_b,
        )

    gathered = {d: {} for d in range(ny)}

    def send_mixed(d):
        gathered[d][0] = mixed[d]
        for s in range(1, ny):
            gathered[(d + s) % ny][s] = moves.y(mixed[d], s)

    def settle(value):
        return line(plain_kernel, [like(value.shape)], value)[0]

    first_norm(0)
    qkv_w[1] = settle(qkv_w[1])
    attend(0)
    send_mixed(0)
    fc1_w[1] = settle(fc1_w[1])
    branch(0)
    fc2_w[1] = settle(fc2_w[1])
    for d in range(1, ny):
        first_norm(d)
        attend(d)
        send_mixed(d)

    hidden, mid = {}, {}

    def to_hidden(d):
        tick(*[gathered[d][s] for s in range(1, ny)])
        hidden[d], mid[d] = line(
            hidden_kernel, [wide, full],
            [gathered[d][s] for s in range(ny)], [out_w[s] for s in range(ny)],
            tok[d], row(out_bias), gain2, shift2,
        )

    act, d_pre, fc1_sums, dmid = {}, {}, {}, {}
    both, all_d = range(CORES), list(range(ny))

    def feed_forward(d):
        act[d], d_pre[d], fc1_sums[d], dmid[d] = line(
            functools.partial(ffn_kernel, min(512, units)),
            [[like((rows, units))] * CORES, [like((rows, units))] * CORES, [like((1, units), F32)] * CORES]
            + [full if d else wide],
            mid[d], d_branch[d], fc1_w, b1, fc2_w,
            scratch=[pltpu.VMEM((rows, width), F32)],
        )

    for d in far:
        to_hidden(d)
        branch(d)
        feed_forward(d)
        dmid[d] = moves.y(dmid[d], -d)
    to_hidden(0)
    feed_forward(0)

    tile = min(512, units)
    steps = units // tile
    swapped = dp_bits[1:2] + dp_bits[:1] + dp_bits[2:]
    tile_bits = [swapped if j % 2 else dp_bits for j in range(steps)]
    fc_sums, fc_got = [], {}

    def ffn_grads(e, j, shares):
        groups = line(
            functools.partial(ffn_grad_kernel, slice(j * tile, (j + 1) * tile), flips(tile_bits[j])),
            [grad_outs(2 * tile, e, shares)],
            [act[d][e] for d in all_d], [d_pre[d][e] for d in all_d],
            [d_branch[d] for d in all_d], [mid[d] for d in all_d], [] if e else fc_got[j],
        )[0]
        if e:
            fc_got[j] = [moves.core(v) for v in groups[0]]
        else:
            fc_sums.append(scatter(groups, tile_bits[j], shares))

    dec_bits = moves.bits("mp")
    dec_shape = like((n_mp // 2, width // n_mp, dec))
    mlp_keep, mlp_send, (dec_total, dec_send) = line(
        functools.partial(mlp_kernel, moves.order("mp")),
        [wide, [full] * (ny - 1), [dec_shape] * 2],
        fc2_w, [act[d] for d in all_d], hidden[0], row(fc2_bias), [grad[d] for d in all_d],
        limit=24, scratch=[pltpu.VMEM((ny * rows, width), BF16)],
    )
    dec_got = moves.flip(dec_send, "mp", dec_bits[0])

    d_hidden, d_attn_own, small2 = line(
        mid_back_kernel, [wide, full, like((4, width), F32)],
        dmid[0], [dmid[d] for d in range(1, ny)], hidden[0], decoded_grad, dec_weight, gain2,
    )
    d_attn = {0: d_attn_own}
    for s in range(1, ny):
        d_attn[s] = moves.y(d_attn_own, s)
    for bit in dec_bits[1:]:
        shape = like((dec_total.shape[0] // 2,) + dec_total.shape[1:])
        dec_total, dec_send = line(fold_kernel, [shape, shape], dec_total, [dec_got])
        if bit != dec_bits[-1]:
            dec_got = moves.flip(dec_send, "mp", bit)
    for e in (1, 0):
        for j in range(steps):
            ffn_grads(e, j, [1, 1])

    dqkv, dn, qv_terms, small_terms = {}, {}, {}, {}

    def attn_back(d, after=()):
        dqkv[d], qv_terms[d], small_terms[d], dn[d] = line(
            functools.partial(attn_bwd_kernel, seq),
            [like((3, rows, CORES * cols)), like((2, CORES * cols), F32), like((2, width), F32)]
            + [full if d else wide],
            counts[d], d_attn[d], qkv[d], [w[0] for w in out_w[0]], qkv_w, normed[d],
            scratch=[pltpu.VMEM((rows, CORES * cols), BF16), pltpu.VMEM((rows, width), F32)], after=after,
        )

    attn_back(0)
    held = lax.optimization_barrier((dec_send, dqkv[0]))
    dec_got = moves.flip(held[0], "mp", dec_bits[-1])
    for d in far:
        attn_back(d)

    def last_grads(e, shares, got=()):
        return line(
            functools.partial(grad_kernel, e, flips(), (0, 1, 2)), [grad_outs(4 * cols, e, shares)],
            [dqkv[d] for d in all_d], [normed[d] for d in all_d],
            [mixed[d] for d in all_d], [d_attn[d] for d in all_d], list(got),
        )[0]

    small, small_send = line(
        small_kernel, [like((8, width), F32)] * 2,
        small2, [small_terms[d] for d in all_d], [[fc1_sums[d][e] for d in all_d] for e in both],
        [qv_terms[d] for d in all_d], after=[dec_got],
    )
    got = moves.core(small_send)
    send = last_grads(1, [1])[0]
    (small,) = line(add_kernel, [like(small.shape, F32)], small, got)
    got = moves.flip(small[:6], "mp", moves.bits("mp")[1])
    fc_sums[0].step()
    (small,) = line(some_rows_kernel, [like(small.shape, F32)], small, got)
    for bit in moves.bits("mp")[2:]:
        got = moves.flip(small[:6], "mp", bit)
        (small,) = line(some_rows_kernel, [like(small.shape, F32)], small, got)
    dec_rows = dec_total.shape[1]
    (mix,) = line(mix_kernel, [like((dec_rows + 4 * small.shape[0], dec))], dec_total, dec_got, small)
    mix_todo = dp_bits[::-1]
    mix_got = moves.flip(mix, "dp", mix_todo.pop(0))

    def mix_step():
        nonlocal mix, mix_got
        (mix,) = line(functools.partial(mix_add_kernel, dec_rows), [like(mix.shape)], mix, mix_got)
        mix_got = moves.flip(mix, "dp", mix_todo.pop(0))

    for s in fc_sums[1:]:
        s.step()
    *held, _ = lax.optimization_barrier((*send, fc_sums[-1].keep))
    crossed = [moves.core(v) for v in held]
    for d in range(1, ny):
        (send,) = line(plain_kernel, [full], dn[d])
        dn[d] = moves.y(send, -d)
    last_sum = scatter(last_grads(0, [9, 7], crossed), dp_bits, [9, 7], start=False)
    last_fc = last_steps(fc_sums)
    mix_step()
    last_sum.start_after(mix)
    terms = [dn[d] for d in range(1, ny)]
    (grad_tokens,) = line(token_back_kernel, [full], dn[0], terms, tokens, d_hidden, gain1, final=True)
    while mix_todo:
        mix_step()
    last_sum.step()
    dec_total, small = line(
        functools.partial(mix_end_kernel, dec_rows), [like((1, dec_rows, dec)), like(small.shape, F32)], mix, mix_got
    )
    fc1_grad, fc2_grad = finish(
        last_fc,
        [(slice_cols, units), (units, slice_cols)],
        [[(1, False, (j * tile, None)), (0, True, (None, j * tile))] for j in range(steps)],
    )
    mlp_far = []
    for d in range(1, ny):
        (send,) = line(plain_kernel, [full], mlp_send[d - 1])
        mlp_far.append(moves.y(send, -d))
    dec_bits_back = list(reversed(dec_bits))
    for bit in dec_bits_back[:-1]:
        dec_got = moves.flip(dec_total, "mp", bit)
        shape = (2 * dec_total.shape[0],) + dec_total.shape[1:]
        (dec_total,) = line(stack_kernel, [like(shape)], dec_total, dec_got)
    dec_got = moves.flip(dec_total, "mp", dec_bits_back[-1])
    while last_sum.bits:
        last_sum.step()
    (grad_dec_weight,) = line(
        functools.partial(place_kernel, "mp"), [[like((width, dec), F32)]], dec_total, dec_got, final=True,
        scratch=[pltpu.VMEM((n_mp, width // n_mp, dec), BF16)],
    )[0]
    (latent,) = line(latent_kernel, [full], mlp_keep, mlp_far, final=True)
    norm1_shift_grad = small[5]
    norm1_gain_grad = (small[4] - norm1_shift * norm1_shift_grad) / norm1_gain
    grad_qv_bias = small[7, : 2 * cols].reshape(2, cols)
    grad_qkv_weight, grad_out_weight = finish(
        ([last_sum.keep], last_sum.got),
        [(3, slice_cols, cols), (cols, slice_cols)],
        [[(0, True, 0), (0, True, 1), (0, True, 2), (1, False, (0, None))]],
    )
    return (
        latent,
        grad_tokens,
        norm1_gain_grad,
        norm1_shift_grad,
        grad_qkv_weight,
        grad_qv_bias,
        grad_out_weight,
        small[2],
        small[0],
        small[1],
        fc1_grad,
        small[6, :units],
        fc2_grad,
        small[3],
        grad_dec_weight,
    )


def solution(mesh):
    return jax.shard_map(
        shards,
        mesh=mesh,
        in_specs=(
            P(("dp", "mp"), None),
            P("dp"),
            P(),
            P(),
            P(None, None, "mp"),
            P(None, "mp"),
            P("mp", None),
            P(),
            P(),
            P(),
            P(None, "mp"),
            P("mp"),
            P("mp", None),
            P(),
            P(),
            P(("dp", "mp"), None),
        ),
        out_specs=(
            P(("dp", "mp"), None),
            P(("dp", "mp"), None),
            P(),
            P(),
            P(None, "dp", "mp"),
            P(None, "mp"),
            P("mp", "dp"),
            P(),
            P(),
            P(),
            P("dp", "mp"),
            P("mp"),
            P("mp", "dp"),
            P(),
            P(),
        ),
        check_vma=False,
    )
```
